128 devices in a mesh: grp: 16 (over z, y), inner: 8 (over x, core).
Axes of the slice: x: 4, y: 4, z: 4, core: 2. Of those that a mesh axis runs over, the one named last changes fastest.
Arguments:
- grid_in: bfloat16 [262144, 474], P(('grp', 'inner')), may hold values from -6 to 6
- g2m_geom: float32 [4, 524288], P(None, ('grp', 'inner')), may hold values from -6 to 6
- g2m_src: int32 [524288], P(('grp', 'inner')), may hold values from 0 to 2047
- g2m_dst: int32 [524288, 1], P(('grp', 'inner')), may hold values from 0 to 127, as said below
- g2m_node: int32 [524288], P(('grp', 'inner')), may hold values from 0 to 319
- mesh_emb: bfloat16 [40960, 512], P(('grp', 'inner')), may hold values from -6 to 6
- mesh_send: int32 [327680], P(('grp', 'inner')), may hold values from 0 to 3199
- mesh_recv: int32 [327680], P(('grp', 'inner')), may hold values from 0 to 319
- w_in1: bfloat16 [474, 512], replicated, may hold values from -0.25 to 0.25
- b_in: float32 [512], replicated, may hold values from -3 to 3
- w_in2: bfloat16 [512, 512], replicated, may hold values from -0.25 to 0.25
- w_g2m: bfloat16 [512, 512], replicated, may hold values from -0.25 to 0.25
- w_geo: float32 [4, 512], replicated, may hold values from -3 to 3
- b_g2m: float32 [512], replicated, may hold values from -3 to 3
- w_enc1: bfloat16 [512, 512], replicated, may hold values from -0.125 to 0.125
- b_enc: float32 [512], replicated, may hold values from -3 to 3
- w_enc2: bfloat16 [512, 512], replicated, may hold values from -0.25 to 0.25
- w_snd: bfloat16 [512, 512], replicated, may hold values from -0.25 to 0.25
- w_rcv: bfloat16 [512, 512], replicated, may hold values from -0.25 to 0.25
- b_edge: float32 [512], replicated, may hold values from -3 to 3
- w_edge: bfloat16 [512, 512], replicated, may hold values from -0.25 to 0.25
- w_p1: bfloat16 [512, 512], replicated, may hold values from -0.125 to 0.125
- w_p2: bfloat16 [512, 512], replicated, may hold values from -0.25 to 0.25
- b_p: float32 [512], replicated, may hold values from -3 to 3
- w_p3: bfloat16 [512, 512], replicated, may hold values from -0.25 to 0.25
Outputs:
- mesh_out: bfloat16 [40960, 512], P(('grp', 'inner'))
The draws below stay inside these ranges and needn't reach their ends.
Inputs may be any that keep to these rules, and one draw needn't show every extreme that they name: `g2m_src`: grid node of an edge within its own block of 2048 rows. `g2m_dst`: an edge of band b names a band from b - 2 to b + 2; in each aligned block of 4096 edges (the edges of one band) the band itself is named exactly 2048 times and no other band more than 2048 times. `mesh_send`: coded sender as in the reference program.
All inputs are finite; a program needn't handle non-finite values.
Results may differ from the reference program's by a relative error of at most 0.02.
Values may be sent and summed in bfloat16 or wider, within the bound.
No kernel may reach another device: no remote copies, remote signals or barrier semaphores. Data moves between devices by JAX's collectives and lax.ppermute only.
A program may use at most 64 MiB of HBM per device.

```python
import jax
import jax.numpy as jnp
from jax import lax

D = 512
CIN = 474
G_DEV = 2048
M_DEV = 320
G2M_DEV = 4096
ME_DEV = 2560
CAP = 2048
GRID = 262144
MESH = 40960
G2M = 524288
ME = 327680
N_GRP = 16
N_INNER = 8
DEVICES = 128


def draw_g2m_dst(key, part):
    key = jax.random.fold_in(key, 11)
    perm_key, step_key = jax.random.split(key)
    band_keys = jax.random.split(perm_key, DEVICES)
    orders = jax.vmap(lambda k: jax.random.permutation(k, G2M_DEV))(band_keys).astype(jnp.int32)
    own = orders < CAP
    pick = jax.random.randint(step_key, (DEVICES, G2M_DEV), 0, 4, dtype=jnp.int32)
    offset = jnp.where(pick < 2, pick - 2, pick - 1)
    band = jnp.arange(DEVICES, dtype=jnp.int32)[:, None]
    moved = band + offset
    inside = (moved >= 0) & (moved < DEVICES)
    moved = jnp.where(inside, moved, band - offset)
    target = jnp.where(own, band, moved)
    return target.reshape(G2M, 1).astype(jnp.int32)


def plant(array, rng, smallest, top_value):
    longest = array.shape.index(max(array.shape))
    spots = []
    for shift in (0, 1):
        where = [jax.random.randint(jax.random.fold_in(rng, axis), (), 0, length) for axis, length in enumerate(array.shape)]
        where[longest] = (where[longest] + shift) % array.shape[longest]
        spots.append(tuple(where))
    return array.at[spots[0]].set(smallest).at[spots[1]].set(top_value)


def block_levels(own_key, dims, cuts, smallest, top_value):
    factor_of, own = 1.0, jax.random.fold_in(own_key, 6)
    for axis_at, blocks in cuts:
        heights = jnp.exp(jax.random.uniform(jax.random.fold_in(own, axis_at), (blocks,), jnp.float32, smallest / len(cuts), top_value / len(cuts)))
        factor_of = factor_of * jnp.repeat(heights, dims[axis_at] // blocks).reshape([-1 if axis == axis_at else 1 for axis in range(len(dims))])
    return factor_of


def gaussian(key, extent, scale, most, pieces=(), held_as=jnp.bfloat16):
    result = scale * jax.random.normal(key, extent, jnp.float32)
    if pieces:
        result = result * block_levels(key, extent, pieces, -0.22, 0.18)
    return jnp.clip(result, -most, most).astype(held_as)


def setup_inputs(seed: int = 0) -> dict:
    streams_of = jax.random.split(jax.random.key(seed), 26)
    return {
        "grid_in": gaussian(streams_of[0], (GRID, CIN), 1.0, 6.0, ((0, 128),)),
        "g2m_geom": gaussian(streams_of[1], (4, G2M), 1.0, 6.0, ((1, 128),), jnp.float32),
        "g2m_src": plant(jax.random.randint(streams_of[2], (G2M,), 0, G_DEV), jax.random.fold_in(streams_of[2], 1), 0, G_DEV - 1).astype(jnp.int32),
        "g2m_dst": draw_g2m_dst(jax.random.fold_in(streams_of[25], 71), 0),
        "g2m_node": plant(jax.random.randint(streams_of[4], (G2M,), 0, M_DEV), jax.random.fold_in(streams_of[4], 1), 0, M_DEV - 1).astype(jnp.int32),
        "mesh_emb": gaussian(streams_of[5], (MESH, D), 1.0, 6.0, ((0, 128),)),
        "mesh_send": plant(jax.random.randint(streams_of[6], (ME,), 0, (N_INNER + 2) * M_DEV), jax.random.fold_in(streams_of[6], 1), 0, ((N_INNER + 2) * M_DEV) - 1).astype(jnp.int32),
        "mesh_recv": plant(jax.random.randint(streams_of[7], (ME,), 0, M_DEV), jax.random.fold_in(streams_of[7], 1), 0, M_DEV - 1).astype(jnp.int32),
        "w_in1": gaussian(streams_of[8], (CIN, D), CIN ** -0.5, 0.25),
        "b_in": gaussian(streams_of[9], (D,), 0.5, 3.0, (), jnp.float32),
        "w_in2": gaussian(streams_of[10], (D, D), D ** -0.5, 0.25),
        "w_g2m": gaussian(streams_of[11], (D, D), D ** -0.5, 0.25),
        "w_geo": gaussian(streams_of[12], (4, D), 4 ** -0.5, 3.0, (), jnp.float32),
        "b_g2m": gaussian(streams_of[13], (D,), 0.5, 3.0, (), jnp.float32),
        "w_enc1": gaussian(streams_of[14], (D, D), (4 * D) ** -0.5, 0.125),
        "b_enc": gaussian(streams_of[15], (D,), 0.5, 3.0, (), jnp.float32),
        "w_enc2": gaussian(streams_of[16], (D, D), D ** -0.5, 0.25),
        "w_snd": gaussian(streams_of[17], (D, D), D ** -0.5, 0.25),
        "w_rcv": gaussian(streams_of[18], (D, D), D ** -0.5, 0.25),
        "b_edge": gaussian(streams_of[19], (D,), 0.5, 3.0, (), jnp.float32),
        "w_edge": gaussian(streams_of[20], (D, D), D ** -0.5, 0.25),
        "w_p1": gaussian(streams_of[21], (D, D), (4 * D) ** -0.5, 0.125),
        "w_p2": gaussian(streams_of[22], (D, D), D ** -0.5, 0.25),
        "b_p": gaussian(streams_of[23], (D,), 0.5, 3.0, (), jnp.float32),
        "w_p3": gaussian(streams_of[24], (D, D), D ** -0.5, 0.25),
    }


def reference(grid_in, g2m_geom, g2m_src, g2m_dst, g2m_node, mesh_emb, mesh_send, mesh_recv, w_in1, b_in, w_in2, w_g2m, w_geo, b_g2m, w_enc1, b_enc, w_enc2, w_snd, w_rcv, b_edge, w_edge, w_p1, w_p2, b_p, w_p3):
    grid_hid = jax.nn.silu(jnp.dot(grid_in, w_in1, preferred_element_type=jnp.float32) + b_in).astype(jnp.bfloat16)
    grid_lat = jnp.dot(grid_hid, w_in2, preferred_element_type=jnp.float32).astype(jnp.bfloat16)
    blocks = jnp.arange(G2M, dtype=jnp.int32) // G2M_DEV
    picked = grid_lat[g2m_src + G_DEV * blocks]
    geom_term = jnp.dot(g2m_geom.T, w_geo, precision=lax.Precision.HIGHEST)
    msg = jax.nn.silu(jnp.dot(picked, w_g2m, preferred_element_type=jnp.float32) + geom_term + b_g2m).astype(jnp.bfloat16)
    target = g2m_dst[:, 0] * M_DEV + g2m_node
    agg_g = jax.ops.segment_sum(msg.astype(jnp.float32), target, num_segments=MESH).astype(jnp.bfloat16)
    enc = jax.nn.silu(jnp.dot(agg_g, w_enc1, preferred_element_type=jnp.float32) + b_enc).astype(jnp.bfloat16)
    mesh_lat = (mesh_emb.astype(jnp.float32) + jnp.dot(enc, w_enc2, preferred_element_type=jnp.float32)).astype(jnp.bfloat16)
    senders = jnp.dot(mesh_lat, w_snd, preferred_element_type=jnp.float32).astype(jnp.bfloat16)
    receivers = jnp.dot(mesh_lat, w_rcv, preferred_element_type=jnp.float32).astype(jnp.bfloat16)
    eblock = jnp.arange(ME, dtype=jnp.int32) // ME_DEV
    group = eblock // N_INNER
    place = eblock % N_INNER
    coded = mesh_send
    width = N_INNER * M_DEV
    in_group = group * width + coded
    lower = ((group - 1) * N_INNER + place) * M_DEV + (coded - width)
    upper = ((group + 1) * N_INNER + place) * M_DEV + (coded - width - M_DEV)
    node_id = jnp.where(coded < width, in_group, jnp.where(coded < width + M_DEV, lower, upper))
    valid = (coded < width) | ((coded >= width) & (coded < width + M_DEV) & (group > 0)) | ((coded >= width + M_DEV) & (group < N_GRP - 1))
    send_rows = jnp.where(valid[:, None], senders[jnp.clip(node_id, 0, MESH - 1)], jnp.zeros((), jnp.bfloat16))
    recv_id = eblock * M_DEV + mesh_recv
    edge_hid = jax.nn.silu(send_rows.astype(jnp.float32) + receivers[recv_id].astype(jnp.float32) + b_edge).astype(jnp.bfloat16)
    edge_lat = jnp.dot(edge_hid, w_edge, preferred_element_type=jnp.float32).astype(jnp.bfloat16)
    agg_m = jax.ops.segment_sum(edge_lat.astype(jnp.float32), recv_id, num_segments=MESH).astype(jnp.bfloat16)
    node_hid = jax.nn.silu(jnp.dot(agg_m, w_p1, preferred_element_type=jnp.float32) + jnp.dot(mesh_lat, w_p2, preferred_element_type=jnp.float32) + b_p).astype(jnp.bfloat16)
    return (mesh_lat.astype(jnp.float32) + jnp.dot(node_hid, w_p3, preferred_element_type=jnp.float32)).astype(jnp.bfloat16)
```

```python
import jax
import jax.numpy as jnp
from jax import lax
from jax.experimental import pallas as pl
from jax.experimental.pallas import tpu as pltpu
from jax.sharding import PartitionSpec as P

F32 = jnp.float32
BF16 = jnp.bfloat16
LANES = 128
EDGE_BLOCK = 256
BOTH = ("grp", "inner")
VMEM_BYTES = 48 * 2**20


def silu(v):
    half = v * 0.5
    return half + half * jnp.tanh(half)


def split3(v):
    high = v.astype(BF16).astype(F32)
    rest = v - high
    mid = rest.astype(BF16).astype(F32)
    return high, mid, (rest - mid).astype(BF16).astype(F32)


def dot(a, b):
    return jnp.dot(a, b, preferred_element_type=F32)


def put_rows(table, first, rows):
    parts = rows.shape[1] // LANES
    for j in range(parts):
        table[pl.ds(first * parts + j, rows.shape[0], stride=parts), :] = rows[
            :, j * LANES : (j + 1) * LANES
        ]


def message_kernel(
    src, grid_in, w_in1, b_in, w_in2, w_g2m, geom, w_geo, b_g2m, msg, table, buf_a, buf_b, w8, g8, w48
):
    w_both = dot(w_in2[...], w_g2m[...]).astype(BF16)
    w8[...] = jnp.zeros_like(w8)
    w8[0:4, :] = w_geo[...]
    w8[4:5, :] = b_g2m[...]
    high, mid, low = split3(w8[...])
    w48[...] = jnp.concatenate([high, high, high, mid, mid, low], axis=0).astype(BF16)
    g8[...] = jnp.zeros_like(g8)
    g8[0:4, :] = geom[...]
    g8[4:5, :] = jnp.ones((1, g8.shape[1]), F32)
    for k in range(grid_in.shape[0] // 256):
        hid = silu(dot(grid_in[k * 256 : (k + 1) * 256, :], w_in1[...]) + b_in[...]).astype(BF16)
        put_rows(table, k * 256, dot(hid, w_both))

    def gather(base, buf):
        for e in range(EDGE_BLOCK):
            row = pl.multiple_of(src[base + e] * 4, 4)
            buf[4 * e : 4 * e + 4, :] = table[pl.ds(row, 4), :]

    def emit(base, buf):
        base = pl.multiple_of(base, EDGE_BLOCK)
        high, mid, low = split3(g8[:, pl.ds(base, EDGE_BLOCK)])
        g48 = jnp.concatenate([high, mid, low, high, mid, high], axis=0).astype(BF16)
        geo = lax.dot_general(g48, w48[...], (((0,), (0,)), ((), ())), preferred_element_type=F32)
        for j in range(4):
            v = buf[pl.ds(j, EDGE_BLOCK, stride=4), :] + geo[:, j * LANES : (j + 1) * LANES]
            msg[pl.ds(base, EDGE_BLOCK), j * LANES : (j + 1) * LANES] = silu(v).astype(BF16)

    blocks = msg.shape[0] // EDGE_BLOCK
    gather(0, buf_a)

    def step(t, carry):
        base = t * (2 * EDGE_BLOCK)
        gather(base + EDGE_BLOCK, buf_b)
        emit(base, buf_a)
        gather(jnp.minimum(base + 2 * EDGE_BLOCK, (blocks - 1) * EDGE_BLOCK), buf_a)
        emit(base + EDGE_BLOCK, buf_b)
        return carry

    lax.fori_loop(0, blocks // 2, step, 0)


def messages(g2m_src, grid_in, w_in1, b_in, w_in2, w_g2m, geom, w_geo, b_g2m):
    edges, nodes, width = g2m_src.shape[0], grid_in.shape[0], w_in1.shape[1]
    vmem = pl.BlockSpec(memory_space=pltpu.VMEM)
    return pl.pallas_call(
        message_kernel,
        out_shape=jax.ShapeDtypeStruct((edges, width), BF16),
        in_specs=[pl.BlockSpec(memory_space=pltpu.SMEM)] + [vmem] * 8,
        out_specs=vmem,
        scratch_shapes=[
            pltpu.VMEM((4 * nodes, LANES), F32),
            pltpu.VMEM((4 * EDGE_BLOCK, LANES), F32),
            pltpu.VMEM((4 * EDGE_BLOCK, LANES), F32),
            pltpu.VMEM((8, width), F32),
            pltpu.VMEM((8, edges), F32),
            pltpu.VMEM((48, width), BF16),
        ],
        compiler_params=pltpu.CompilerParams(vmem_limit_bytes=VMEM_BYTES),
        name="messages",
    )(g2m_src, grid_in, w_in1, b_in.reshape(1, -1), w_in2, w_g2m, geom, w_geo, b_g2m.reshape(1, -1))


def encoder_kernel(own, near, one, two, emb, w_enc1, b_enc, w_enc2, w_snd, w_rcv, b_edge, lat, snd, rcv):
    total = own[...] + near[...].astype(F32) + one[...].astype(F32) + two[...].astype(F32)
    enc = silu(dot(total.astype(BF16), w_enc1[...]) + b_enc[...]).astype(BF16)
    mesh_lat = (emb[...].astype(F32) + dot(enc, w_enc2[...])).astype(BF16)
    lat[...] = mesh_lat
    snd[...] = dot(mesh_lat, w_snd[...]).astype(BF16)
    rcv[...] = dot(mesh_lat, w_rcv[...]) + b_edge[...]


def encoder(own, near, one, two, emb, w_enc1, b_enc, w_enc2, w_snd, w_rcv, b_edge):
    vmem = pl.BlockSpec(memory_space=pltpu.VMEM)
    rows, width = emb.shape
    return pl.pallas_call(
        encoder_kernel,
        out_shape=[
            jax.ShapeDtypeStruct((rows, width), BF16),
            jax.ShapeDtypeStruct((rows, width), BF16),
            jax.ShapeDtypeStruct((rows, width), F32),
        ],
        in_specs=[vmem] * 11,
        out_specs=[vmem] * 3,
        compiler_params=pltpu.CompilerParams(vmem_limit_bytes=VMEM_BYTES),
        name="encoder",
    )(own, near, one, two, emb, w_enc1, b_enc.reshape(1, -1), w_enc2, w_snd, w_rcv, b_edge.reshape(1, -1))


def processor_kernel(
    place, send, recv, *refs
):
    shards = refs[:10]
    rcv, recv_row, lat, w_edge, w_p1, w_p2, b_p, w_p3, out, table, rtable, buf_a, buf_b, hid = refs[10:]
    rows = lat.shape[0]
    for k in range(10):
        put_rows(table, place[k], shards[k][...].astype(F32))
    put_rows(rtable, 0, rcv[...])

    def gather(base, buf):
        for e in range(EDGE_BLOCK):
            s = pl.multiple_of(send[base + e] * 4, 4)
            r = pl.multiple_of(recv[base + e] * 4, 4)
            buf[4 * e : 4 * e + 4, :] = table[pl.ds(s, 4), :] + rtable[pl.ds(r, 4), :]

    def emit(base, buf):
        base = pl.multiple_of(base, EDGE_BLOCK)
        for j in range(4):
            v = buf[pl.ds(j, EDGE_BLOCK, stride=4), :]
            hid[pl.ds(base, EDGE_BLOCK), j * LANES : (j + 1) * LANES] = silu(v).astype(BF16)

    blocks = hid.shape[0] // EDGE_BLOCK
    gather(0, buf_a)

    def step(t, carry):
        base = t * (2 * EDGE_BLOCK)
        gather(base + EDGE_BLOCK, buf_b)
        emit(base, buf_a)
        gather(jnp.minimum(base + 2 * EDGE_BLOCK, (blocks - 1) * EDGE_BLOCK), buf_a)
        emit(base + EDGE_BLOCK, buf_b)
        return carry

    lax.fori_loop(0, blocks // 2, step, 0)
    ids = lax.broadcasted_iota(jnp.int32, (rows, hid.shape[0]), 0)
    select = jnp.where(ids == recv_row[...], 1.0, 0.0).astype(BF16)
    agg = dot(dot(select, hid[...]).astype(BF16), w_edge[...]).astype(BF16)
    mesh_lat = lat[...]
    node = silu(dot(agg, w_p1[...]) + dot(mesh_lat, w_p2[...]) + b_p[...]).astype(BF16)
    out[...] = (mesh_lat.astype(F32) + dot(node, w_p3[...])).astype(BF16)


def processor(place, send, recv, shards, rcv, lat, w_edge, w_p1, w_p2, b_p, w_p3):
    vmem = pl.BlockSpec(memory_space=pltpu.VMEM)
    smem = pl.BlockSpec(memory_space=pltpu.SMEM)
    rows, width = lat.shape
    edges = send.shape[0]
    return pl.pallas_call(
        processor_kernel,
        out_shape=jax.ShapeDtypeStruct((rows, width), BF16),
        in_specs=[smem] * 3 + [vmem] * 18,
        out_specs=vmem,
        scratch_shapes=[
            pltpu.VMEM((4 * 10 * rows, LANES), F32),
            pltpu.VMEM((4 * rows, LANES), F32),
            pltpu.VMEM((4 * EDGE_BLOCK, LANES), F32),
            pltpu.VMEM((4 * EDGE_BLOCK, LANES), F32),
            pltpu.VMEM((edges, width), BF16),
        ],
        compiler_params=pltpu.CompilerParams(vmem_limit_bytes=VMEM_BYTES),
        name="processor",
    )(
        place, send, recv, *shards, rcv, recv.reshape(1, -1), lat, w_edge, w_p1, w_p2, b_p.reshape(1, -1), w_p3
    )


def on_device(
    grid_in,
    g2m_geom,
    g2m_src,
    g2m_dst,
    g2m_node,
    mesh_emb,
    mesh_send,
    mesh_recv,
    w_in1,
    b_in,
    w_in2,
    w_g2m,
    w_geo,
    b_g2m,
    w_enc1,
    b_enc,
    w_enc2,
    w_snd,
    w_rcv,
    b_edge,
    w_edge,
    w_p1,
    w_p2,
    b_p,
    w_p3,
):
    groups, places = lax.axis_size("grp"), lax.axis_size("inner")
    bands = groups * places
    nodes_here = mesh_emb.shape[0]
    band = lax.axis_index(BOTH)
    place = lax.axis_index("inner")
    core = place % 2

    def by_parity(even, odd):
        pairs = [(b, b + (odd if b % 2 else even)) for b in range(bands)]
        pairs = [pair for pair in pairs if 0 <= pair[1] < bands]
        return lambda value: lax.ppermute(value, BOTH, pairs)

    def along_x(value, by):
        return lax.ppermute(value, "inner", [(i, (i + 2 * by) % places) for i in range(places)])

    def along_groups(value, by):
        pairs = [(i, i + by) for i in range(groups) if 0 <= i + by < groups]
        return lax.ppermute(value, "grp", pairs)

    other_core = by_parity(1, -1)

    msg = messages(g2m_src, grid_in, w_in1, b_in, w_in2, w_g2m, g2m_geom, w_geo, b_g2m)
    target = (g2m_dst[:, 0] - band + 2) * nodes_here + g2m_node
    node_ids = jnp.arange(nodes_here, dtype=jnp.int32)

    def band_sum(which):
        select = (node_ids[:, None] + which * nodes_here == target[None, :]).astype(BF16)
        return dot(select, msg)

    crossing = other_core(band_sum(jnp.where(core == 0, 1, 3)).astype(BF16))
    two = by_parity(-2, 2)(band_sum(jnp.where(core == 0, 0, 4)).astype(BF16))
    joint = band_sum(jnp.where(core == 0, 4, 0)) + crossing.astype(F32)
    one = by_parity(2, -2)(joint.astype(BF16))
    near = other_core(band_sum(jnp.where(core == 0, 3, 1)).astype(BF16))
    own = band_sum(2)
    mesh_lat, senders, receivers = encoder(
        own, near, one, two, mesh_emb, w_enc1, b_enc, w_enc2, w_snd, w_rcv, b_edge
    )

    right = along_x(senders, 1)
    left = along_x(senders, -1)
    far = along_x(senders, 2)
    low = along_groups(senders, 1)
    high = along_groups(senders, -1)
    shards = [senders, right, left, far]
    shards = shards + [other_core(shard) for shard in shards] + [low, high]
    mine = [place, (place - 2) % places, (place + 2) % places, (place + 4) % places]
    where = mine + [p + 1 - 2 * core for p in mine] + [places, places + 1]
    starts = jnp.stack([jnp.asarray(p, jnp.int32) for p in where]) * nodes_here
    return processor(
        starts, mesh_send, mesh_recv, shards, receivers, mesh_lat, w_edge, w_p1, w_p2, b_p, w_p3
    )


def solution(mesh):
    split = P(BOTH)
    rows = P(BOTH, None)
    return jax.shard_map(
        on_device,
        mesh=mesh,
        in_specs=(rows, P(None, BOTH), split, rows, split, rows, split, split) + (P(),) * 17,
        out_specs=rows,
        check_vma=False,
    )
```

```python
import jax
import jax.numpy as jnp
from jax import lax
from jax.experimental import pallas as pl
from jax.experimental.pallas import tpu as pltpu
from jax.sharding import PartitionSpec as P

F32 = jnp.float32
BF16 = jnp.bfloat16
LANES = 128
EDGE_BLOCK = 256
BOTH = ("grp", "inner")
VMEM_BYTES = 48 * 2**20


def silu(v):
    half = v * 0.5
    return half + half * jnp.tanh(half)


def split3(v):
    high = v.astype(BF16).astype(F32)
    rest = v - high
    mid = rest.astype(BF16).astype(F32)
    return high, mid, (rest - mid).astype(BF16).astype(F32)


def dot(a, b):
    return jnp.dot(a, b, preferred_element_type=F32)


def dot_first(a, b):
    return lax.dot_general(a, b, (((0,), (0,)), ((), ())), preferred_element_type=F32)


def put_rows(table, first, rows):
    parts = rows.shape[1] // LANES
    for j in range(parts):
        table[pl.ds(first * parts + j, rows.shape[0], stride=parts), :] = rows[
            :, j * LANES : (j + 1) * LANES
        ]


def message_kernel(
    src, grid_in, w_in1, b_in, w_in2, w_g2m, geom, w_geo, b_g2m, msg, table, buf_a, buf_b, w8, g8, w48
):
    w_both = dot(w_in2[...], w_g2m[...]).astype(BF16)
    w8[...] = jnp.zeros_like(w8)
    w8[0:4, :] = w_geo[...]
    w8[4:5, :] = b_g2m[...]
    high, mid, low = split3(w8[...])
    w48[...] = jnp.concatenate([high, high, high, mid, mid, low], axis=0).astype(BF16)
    g8[...] = jnp.zeros_like(g8)
    g8[0:4, :] = geom[...]
    g8[4:5, :] = jnp.ones((1, g8.shape[1]), F32)
    for k in range(grid_in.shape[1] // 256):
        hid = dot_first(grid_in[:, k * 256 : (k + 1) * 256], w_in1[...])
        hid = silu(hid + b_in[...]).astype(BF16)
        put_rows(table, k * 256, dot(hid, w_both))

    def gather(base, buf):
        for e in range(EDGE_BLOCK):
            row = pl.multiple_of(src[base + e] * 4, 4)
            buf[4 * e : 4 * e + 4, :] = table[pl.ds(row, 4), :]

    def emit(base, buf):
        base = pl.multiple_of(base, EDGE_BLOCK)
        high, mid, low = split3(g8[:, pl.ds(base, EDGE_BLOCK)])
        g48 = jnp.concatenate([high, mid, low, high, mid, high], axis=0).astype(BF16)
        geo = dot_first(g48, w48[...])
        for j in range(4):
            v = buf[pl.ds(j, EDGE_BLOCK, stride=4), :] + geo[:, j * LANES : (j + 1) * LANES]
            msg[pl.ds(base, EDGE_BLOCK), j * LANES : (j + 1) * LANES] = silu(v).astype(BF16)

    blocks = msg.shape[0] // EDGE_BLOCK
    gather(0, buf_a)

    def step(t, carry):
        base = t * (2 * EDGE_BLOCK)
        gather(base + EDGE_BLOCK, buf_b)
        emit(base, buf_a)
        gather(jnp.minimum(base + 2 * EDGE_BLOCK, (blocks - 1) * EDGE_BLOCK), buf_a)
        emit(base + EDGE_BLOCK, buf_b)
        return carry

    lax.fori_loop(0, blocks // 2, step, 0)


def messages(g2m_src, grid_in, w_in1, b_in, w_in2, w_g2m, geom, w_geo, b_g2m):
    edges, nodes, width = g2m_src.shape[0], grid_in.shape[1], w_in1.shape[1]
    vmem = pl.BlockSpec(memory_space=pltpu.VMEM)
    return pl.pallas_call(
        message_kernel,
        out_shape=jax.ShapeDtypeStruct((edges, width), BF16),
        in_specs=[pl.BlockSpec(memory_space=pltpu.SMEM)] + [vmem] * 8,
        out_specs=vmem,
        scratch_shapes=[
            pltpu.VMEM((4 * nodes, LANES), F32),
            pltpu.VMEM((4 * EDGE_BLOCK, LANES), F32),
            pltpu.VMEM((4 * EDGE_BLOCK, LANES), F32),
            pltpu.VMEM((8, width), F32),
            pltpu.VMEM((8, edges), F32),
            pltpu.VMEM((48, width), BF16),
        ],
        compiler_params=pltpu.CompilerParams(vmem_limit_bytes=VMEM_BYTES),
        name="messages",
    )(g2m_src, grid_in, w_in1, b_in.reshape(1, -1), w_in2, w_g2m, geom, w_geo, b_g2m.reshape(1, -1))


def encoder_kernel(own, near, one, two, emb, w_enc1, b_enc, w_enc2, w_snd, w_rcv, b_edge, lat, snd, rcv):
    total = own[...] + near[...].astype(F32) + one[...].astype(F32) + two[...].astype(F32)
    enc = silu(dot(total.astype(BF16), w_enc1[...]) + b_enc[...]).astype(BF16)
    mesh_lat = (emb[...].astype(F32) + dot(enc, w_enc2[...])).astype(BF16)
    lat[...] = mesh_lat
    snd[...] = dot(mesh_lat, w_snd[...]).astype(BF16)
    rcv[...] = dot(mesh_lat, w_rcv[...]) + b_edge[...]


def encoder(own, near, one, two, emb, w_enc1, b_enc, w_enc2, w_snd, w_rcv, b_edge):
    vmem = pl.BlockSpec(memory_space=pltpu.VMEM)
    rows, width = emb.shape
    return pl.pallas_call(
        encoder_kernel,
        out_shape=[
            jax.ShapeDtypeStruct((rows, width), BF16),
            jax.ShapeDtypeStruct((rows, width), BF16),
            jax.ShapeDtypeStruct((rows, width), F32),
        ],
        in_specs=[vmem] * 11,
        out_specs=[vmem] * 3,
        compiler_params=pltpu.CompilerParams(vmem_limit_bytes=VMEM_BYTES),
        name="encoder",
    )(own, near, one, two, emb, w_enc1, b_enc.reshape(1, -1), w_enc2, w_snd, w_rcv, b_edge.reshape(1, -1))


def processor_kernel(
    place, send, recv, *refs
):
    shards = refs[:10]
    rcv, recv_row, lat, w_edge, w_p1, w_p2, b_p, w_p3, out, table, rtable, buf_a, buf_b, hid = refs[10:]
    rows = lat.shape[0]
    for k in range(10):
        put_rows(table, place[k], shards[k][...].astype(F32))
    put_rows(rtable, 0, rcv[...])

    def gather(base, buf):
        for e in range(EDGE_BLOCK):
            s = pl.multiple_of(send[base + e] * 4, 4)
            r = pl.multiple_of(recv[base + e] * 4, 4)
            buf[4 * e : 4 * e + 4, :] = table[pl.ds(s, 4), :] + rtable[pl.ds(r, 4), :]

    def emit(base, buf):
        base = pl.multiple_of(base, EDGE_BLOCK)
        for j in range(4):
            v = buf[pl.ds(j, EDGE_BLOCK, stride=4), :]
            hid[pl.ds(base, EDGE_BLOCK), j * LANES : (j + 1) * LANES] = silu(v).astype(BF16)

    blocks = hid.shape[0] // EDGE_BLOCK
    gather(0, buf_a)

    def step(t, carry):
        base = t * (2 * EDGE_BLOCK)
        gather(base + EDGE_BLOCK, buf_b)
        emit(base, buf_a)
        gather(jnp.minimum(base + 2 * EDGE_BLOCK, (blocks - 1) * EDGE_BLOCK), buf_a)
        emit(base + EDGE_BLOCK, buf_b)
        return carry

    lax.fori_loop(0, blocks // 2, step, 0)
    ids = lax.broadcasted_iota(jnp.int32, (rows, hid.shape[0]), 0)
    select = jnp.where(ids == recv_row[...], 1.0, 0.0).astype(BF16)
    agg = dot(dot(select, hid[...]).astype(BF16), w_edge[...]).astype(BF16)
    mesh_lat = lat[...]
    node = silu(dot(agg, w_p1[...]) + dot(mesh_lat, w_p2[...]) + b_p[...]).astype(BF16)
    out[...] = (mesh_lat.astype(F32) + dot(node, w_p3[...])).astype(BF16)


def processor(place, send, recv, shards, rcv, lat, w_edge, w_p1, w_p2, b_p, w_p3):
    vmem = pl.BlockSpec(memory_space=pltpu.VMEM)
    smem = pl.BlockSpec(memory_space=pltpu.SMEM)
    rows, width = lat.shape
    edges = send.shape[0]
    return pl.pallas_call(
        processor_kernel,
        out_shape=jax.ShapeDtypeStruct((rows, width), BF16),
        in_specs=[smem] * 3 + [vmem] * 18,
        out_specs=vmem,
        scratch_shapes=[
            pltpu.VMEM((4 * 10 * rows, LANES), F32),
            pltpu.VMEM((4 * rows, LANES), F32),
            pltpu.VMEM((4 * EDGE_BLOCK, LANES), F32),
            pltpu.VMEM((4 * EDGE_BLOCK, LANES), F32),
            pltpu.VMEM((edges, width), BF16),
        ],
        compiler_params=pltpu.CompilerParams(vmem_limit_bytes=VMEM_BYTES),
        name="processor",
    )(
        place, send, recv, *shards, rcv, recv.reshape(1, -1), lat, w_edge, w_p1, w_p2, b_p.reshape(1, -1), w_p3
    )


def on_device(
    grid_in,
    g2m_geom,
    g2m_src,
    g2m_dst,
    g2m_node,
    mesh_emb,
    mesh_send,
    mesh_recv,
    w_in1,
    b_in,
    w_in2,
    w_g2m,
    w_geo,
    b_g2m,
    w_enc1,
    b_enc,
    w_enc2,
    w_snd,
    w_rcv,
    b_edge,
    w_edge,
    w_p1,
    w_p2,
    b_p,
    w_p3,
):
    groups, places = lax.axis_size("grp"), lax.axis_size("inner")
    bands = groups * places
    nodes_here = mesh_emb.shape[0]
    band = lax.axis_index(BOTH)
    place = lax.axis_index("inner")
    core = place % 2

    def by_parity(even, odd):
        pairs = [(b, b + (odd if b % 2 else even)) for b in range(bands)]
        pairs = [pair for pair in pairs if 0 <= pair[1] < bands]
        return lambda value: lax.ppermute(value, BOTH, pairs)

    def onward(value):
        pairs = [(i, (i + (-2 if i % 2 else 2)) % places) for i in range(places)]
        return lax.ppermute(value, "inner", pairs)

    def along_groups(value, by):
        pairs = [(i, i + by) for i in range(groups) if 0 <= i + by < groups]
        return lax.ppermute(value, "grp", pairs)

    other_core = by_parity(1, -1)

    msg = messages(g2m_src, grid_in.T, w_in1, b_in, w_in2, w_g2m, g2m_geom, w_geo, b_g2m)
    offset = (g2m_dst[:, 0] - band) * (1 - 2 * core) + 2
    target = offset * nodes_here + g2m_node
    node_ids = jnp.arange(nodes_here, dtype=jnp.int32)

    def band_sum(which):
        select = (node_ids[:, None] + which * nodes_here == target[None, :]).astype(BF16)
        return dot(select, msg)

    crossing = other_core(band_sum(1).astype(BF16))
    two = by_parity(-2, 2)(band_sum(0).astype(BF16))
    joint = band_sum(4) + crossing.astype(F32)
    one = by_parity(2, -2)(joint.astype(BF16))
    near = other_core(band_sum(3).astype(BF16))
    own = band_sum(2)
    mesh_lat, senders, receivers = encoder(
        own, near, one, two, mesh_emb, w_enc1, b_enc, w_enc2, w_snd, w_rcv, b_edge
    )

    next_a = onward(senders)
    partner = other_core(senders)
    next_b = onward(partner)
    low = along_groups(senders, 1)
    high = along_groups(senders, -1)
    far = onward(next_a)
    shards = [senders, partner, next_a, next_b, far]
    shards = shards + [other_core(shard) for shard in shards[2:]] + [low, high]
    turn = 2 * (1 - 2 * core)
    before, far_back, after, far_on = [(place + turn * by) % places for by in (-1, -2, 1, 2)]
    twin = 1 - 2 * core
    where = [place, place + twin, before, before + twin, far_back]
    where = where + [after + twin, after, far_on + twin, places, places + 1]
    starts = jnp.stack([jnp.asarray(p, jnp.int32) for p in where]) * nodes_here
    return processor(
        starts, mesh_send, mesh_recv, shards, receivers, mesh_lat, w_edge, w_p1, w_p2, b_p, w_p3
    )


def solution(mesh):
    split = P(BOTH)
    rows = P(BOTH, None)
    return jax.shard_map(
        on_device,
        mesh=mesh,
        in_specs=(rows, P(None, BOTH), split, rows, split, rows, split, split) + (P(),) * 17,
        out_specs=rows,
        check_vma=False,
    )
```

```python
import jax
import jax.numpy as jnp
from jax import lax
from jax.experimental import pallas as pl
from jax.experimental.pallas import tpu as pltpu
from jax.sharding import PartitionSpec as P

F32 = jnp.float32
BF16 = jnp.bfloat16
LANES = 128
EDGE_BLOCK = 256
BOTH = ("grp", "inner")
MESSAGE_VMEM = 60 * 2**20


def silu(v):
    half = v * 0.5
    return half + half * jnp.tanh(half)


def split3(v):
    high = v.astype(BF16).astype(F32)
    rest = v - high
    mid = rest.astype(BF16).astype(F32)
    return high, mid, (rest - mid).astype(BF16).astype(F32)


def dot(a, b):
    return jnp.dot(a, b, preferred_element_type=F32)


def dot_first(a, b):
    return lax.dot_general(a, b, (((0,), (0,)), ((), ())), preferred_element_type=F32)


def one_hot(ids, rows):
    numbers = lax.broadcasted_iota(jnp.int32, (rows, ids.shape[1]), 0)
    return jnp.where(numbers == ids, 1.0, 0.0).astype(BF16)


def put_rows(table, first, rows):
    parts = rows.shape[1] // LANES
    for j in range(parts):
        table[pl.ds(first * parts + j, rows.shape[0], stride=parts), :] = rows[
            :, j * LANES : (j + 1) * LANES
        ]


def message_kernel(
    scalars, src_hbm, grid_hbm, w_in1_hbm, b_in_hbm, w_in2_hbm, w_g2m_hbm, geom_hbm, w_geo_hbm, b_g2m_hbm, dst_hbm, node_hbm,
    back2, back1, own, on1, on2,
    src, grid_in, w_in1, b_in, w_in2, w_g2m, geom, w_geo, b_g2m, dst, node, table, buf_a, buf_b, w8, g8, w48, w_both, msg_a, msg_b, sums, sems,
):
    nodes, edges = grid_in.shape[1], src.shape[0]
    bands, rows = 5, own.shape[0]
    chunk = 512
    chunks = nodes // chunk
    here = [
        (w_in1_hbm, w_in1), (b_in_hbm, b_in), (w_in2_hbm, w_in2), (w_g2m_hbm, w_g2m), (src_hbm, src),
        (geom_hbm, geom), (w_geo_hbm, w_geo), (b_g2m_hbm, b_g2m), (dst_hbm, dst), (node_hbm, node),
    ]
    copies = [pltpu.make_async_copy(a, b, sems.at[i]) for i, (a, b) in enumerate(here)]
    grids = []
    for k in range(chunks):
        part = pl.ds(k * chunk, chunk)
        grids.append(
            pltpu.make_async_copy(grid_hbm.at[:, part], grid_in.at[:, part], sems.at[len(here) + k])
        )
    order = [copies[2], copies[3], copies[0], copies[1], grids[0], grids[1]] + copies[4:] + grids[2:]
    for copy in order:
        copy.start()
    copies[2].wait()
    copies[3].wait()
    w_both[...] = dot(w_in2[...], w_g2m[...]).astype(BF16)
    copies[0].wait()
    copies[1].wait()
    for k in range(chunks):
        grids[k].wait()
        hid = dot_first(grid_in[:, k * chunk : (k + 1) * chunk], w_in1[...])
        hid = silu(hid + b_in[...]).astype(BF16)
        put_rows(table, k * chunk, dot(hid, w_both[...]))

    for copy in copies[4:]:
        copy.wait()
    node[...] = ((dst[...] - scalars[0]) * scalars[1] + 2) * scalars[2] + node[...]
    w8[...] = jnp.zeros_like(w8)
    w8[0:4, :] = w_geo[...]
    w8[4:5, :] = b_g2m[...]
    high, mid, low = split3(w8[...])
    w48[...] = jnp.concatenate([high, high, high, mid, mid, low], axis=0).astype(BF16)
    g8[...] = jnp.zeros_like(g8)
    g8[0:4, :] = geom[...]
    g8[4:5, :] = jnp.ones((1, g8.shape[1]), F32)
    sums[...] = jnp.zeros_like(sums)
    msg_b[...] = jnp.zeros_like(msg_b)

    def gather(base, buf):
        for e in range(EDGE_BLOCK):
            row = pl.multiple_of(src[base + e] * 4, 4)
            buf[4 * e : 4 * e + 4, :] = table[pl.ds(row, 4), :]

    def emit(base, half, buf):
        base = pl.multiple_of(base, EDGE_BLOCK)
        high, mid, low = split3(g8[:, pl.ds(base, EDGE_BLOCK)])
        g48 = jnp.concatenate([high, mid, low, high, mid, high], axis=0).astype(BF16)
        geo = dot_first(g48, w48[...])
        for j in range(4):
            lanes = slice(j * LANES, (j + 1) * LANES)
            v = buf[pl.ds(j, EDGE_BLOCK, stride=4), :] + geo[:, lanes]
            (msg_a, msg_b)[half][:, lanes] = silu(v).astype(BF16)

    def scatter(base, half):
        base = pl.multiple_of(jnp.maximum(base, 0), EDGE_BLOCK)
        select = one_hot(node[:, pl.ds(base, EDGE_BLOCK)], bands * rows)
        sums[...] += dot(select, (msg_a, msg_b)[half][...])

    blocks = edges // EDGE_BLOCK
    gather(0, buf_a)

    def step(t, carry):
        base = pl.multiple_of(t * (2 * EDGE_BLOCK), 2 * EDGE_BLOCK)
        gather(base + EDGE_BLOCK, buf_b)
        emit(base, 0, buf_a)
        scatter(base - EDGE_BLOCK, 1)
        gather(jnp.minimum(base + 2 * EDGE_BLOCK, (blocks - 1) * EDGE_BLOCK), buf_a)
        emit(base + EDGE_BLOCK, 1, buf_b)
        scatter(base, 0)
        return carry

    lax.fori_loop(0, blocks // 2, step, 0)
    scatter(edges - EDGE_BLOCK, 1)
    for which, out in enumerate((back2, back1, own, on1, on2)):
        out[...] = sums[which * rows : (which + 1) * rows, :].astype(out.dtype)


def band_sums(scalars, rows, *arrays):
    g2m_src, grid_in, w_in1 = arrays[:3]
    edges, nodes, width = g2m_src.shape[0], grid_in.shape[1], w_in1.shape[1]
    vmem = pl.BlockSpec(memory_space=pltpu.VMEM)
    smem = pl.BlockSpec(memory_space=pltpu.SMEM)
    hbm = pl.BlockSpec(memory_space=pltpu.HBM)
    return pl.pallas_call(
        message_kernel,
        out_shape=[jax.ShapeDtypeStruct((rows, width), dtype) for dtype in (BF16, BF16, F32, BF16, F32)],
        in_specs=[smem] + [hbm] * len(arrays),
        out_specs=[vmem] * 5,
        scratch_shapes=[pltpu.SMEM((edges,), jnp.int32)]
        + [pltpu.VMEM(a.shape, a.dtype) for a in arrays[1:]]
        + [
            pltpu.VMEM((4 * nodes, LANES), F32),
            pltpu.VMEM((4 * EDGE_BLOCK, LANES), F32),
            pltpu.VMEM((4 * EDGE_BLOCK, LANES), F32),
            pltpu.VMEM((8, width), F32),
            pltpu.VMEM((8, edges), F32),
            pltpu.VMEM((48, width), BF16),
            pltpu.VMEM((width, width), BF16),
            pltpu.VMEM((EDGE_BLOCK, width), BF16),
            pltpu.VMEM((EDGE_BLOCK, width), BF16),
            pltpu.VMEM((5 * rows, width), F32),
            pltpu.SemaphoreType.DMA((len(arrays) + 3,)),
        ],
        compiler_params=pltpu.CompilerParams(vmem_limit_bytes=MESSAGE_VMEM),
        name="band_sums",
    )(scalars, *arrays)


def encoder_kernel(own, near, one, two, emb, w_enc1, b_enc, w_enc2, w_snd, lat, snd):
    total = own[...] + near[...].astype(F32) + one[...].astype(F32) + two[...].astype(F32)
    enc = silu(dot(total.astype(BF16), w_enc1[...]) + b_enc[...]).astype(BF16)
    mesh_lat = (emb[...].astype(F32) + dot(enc, w_enc2[...])).astype(BF16)
    lat[...] = mesh_lat
    snd[...] = dot(mesh_lat, w_snd[...]).astype(BF16)


def encoder(own, near, one, two, emb, w_enc1, b_enc, w_enc2, w_snd):
    vmem = pl.BlockSpec(memory_space=pltpu.VMEM)
    rows, width = emb.shape
    return pl.pallas_call(
        encoder_kernel,
        out_shape=[jax.ShapeDtypeStruct((rows, width), BF16)] * 2,
        in_specs=[vmem] * 9,
        out_specs=[vmem] * 2,
        compiler_params=pltpu.CompilerParams(vmem_limit_bytes=16 * 2**20),
        name="encoder",
    )(own, near, one, two, emb, w_enc1, b_enc.reshape(1, -1), w_enc2, w_snd)


def receiver_kernel(recv, lat, w_rcv, w_edge, w_p1, w_p2, b_p, recv_rows, w_ep, lat_p2):
    receivers = dot(lat[...], w_rcv[...]).astype(BF16)
    for k in range(recv_rows.shape[0] // 512):
        part = slice(k * 512, (k + 1) * 512)
        select = one_hot(recv[:, part], lat.shape[0])
        recv_rows[part, :] = dot_first(select, receivers).astype(BF16)
    w_ep[...] = dot(w_edge[...], w_p1[...]).astype(BF16)
    lat_p2[...] = dot(lat[...], w_p2[...]) + b_p[...]


def receiver_side(recv, lat, w_rcv, w_edge, w_p1, w_p2, b_p):
    vmem = pl.BlockSpec(memory_space=pltpu.VMEM)
    rows, width = lat.shape
    edges = recv.shape[0]
    return pl.pallas_call(
        receiver_kernel,
        out_shape=[
            jax.ShapeDtypeStruct((edges, width), BF16),
            jax.ShapeDtypeStruct((width, width), BF16),
            jax.ShapeDtypeStruct((rows, width), F32),
        ],
        in_specs=[vmem] * 7,
        out_specs=[vmem] * 3,
        compiler_params=pltpu.CompilerParams(vmem_limit_bytes=16 * 2**20),
        cost_estimate=pl.CostEstimate(flops=2 * 10**9, bytes_accessed=6 * 10**6, transcendentals=0),
        name="receiver_side",
    )(recv.reshape(1, -1), lat, w_rcv, w_edge, w_p1, w_p2, b_p.reshape(1, -1))


def processor_kernel(place, send, recv, b_edge, recv_rows, lat, lat_p2, w_ep, w_p3, *refs):
    shards = refs[:10]
    out, table, buf_a, buf_b, hid, agg = refs[10:]
    rows = lat.shape[0]
    for k in range(10):
        put_rows(table, place[k], shards[k][...].astype(F32))
    agg[...] = jnp.zeros_like(agg)

    def gather(base, buf):
        for e in range(EDGE_BLOCK):
            row = pl.multiple_of(send[base + e] * 4, 4)
            buf[4 * e : 4 * e + 4, :] = table[pl.ds(row, 4), :]

    def emit(base, half, buf):
        base = pl.multiple_of(base, EDGE_BLOCK)
        for j in range(4):
            lanes = slice(j * LANES, (j + 1) * LANES)
            v = buf[pl.ds(j, EDGE_BLOCK, stride=4), :] + b_edge[:, lanes]
            v = v + recv_rows[pl.ds(base, EDGE_BLOCK), lanes].astype(F32)
            hid[half * EDGE_BLOCK : (half + 1) * EDGE_BLOCK, lanes] = silu(v).astype(BF16)

    blocks = send.shape[0] // EDGE_BLOCK
    gather(0, buf_a)

    def step(t, carry):
        base = pl.multiple_of(t * (2 * EDGE_BLOCK), 2 * EDGE_BLOCK)
        gather(base + EDGE_BLOCK, buf_b)
        emit(base, 0, buf_a)
        gather(jnp.minimum(base + 2 * EDGE_BLOCK, (blocks - 1) * EDGE_BLOCK), buf_a)
        emit(base + EDGE_BLOCK, 1, buf_b)
        agg[...] += dot(one_hot(recv[:, pl.ds(base, 2 * EDGE_BLOCK)], rows), hid[...])
        return carry

    lax.fori_loop(0, blocks // 2, step, 0)
    node = silu(dot(agg[...].astype(BF16), w_ep[...]) + lat_p2[...]).astype(BF16)
    out[...] = (lat[...].astype(F32) + dot(node, w_p3[...])).astype(BF16)


def processor(place, send, recv, b_edge, recv_rows, lat, lat_p2, w_ep, w_p3, shards):
    vmem = pl.BlockSpec(memory_space=pltpu.VMEM)
    smem = pl.BlockSpec(memory_space=pltpu.SMEM)
    rows, width = lat.shape
    return pl.pallas_call(
        processor_kernel,
        out_shape=jax.ShapeDtypeStruct((rows, width), BF16),
        in_specs=[smem] * 2 + [vmem] * (7 + len(shards)),
        out_specs=vmem,
        scratch_shapes=[
            pltpu.VMEM((4 * 10 * rows, LANES), F32),
            pltpu.VMEM((4 * EDGE_BLOCK, LANES), F32),
            pltpu.VMEM((4 * EDGE_BLOCK, LANES), F32),
            pltpu.VMEM((2 * EDGE_BLOCK, width), BF16),
            pltpu.VMEM((rows, width), F32),
        ],
        compiler_params=pltpu.CompilerParams(vmem_limit_bytes=24 * 2**20),
        name="processor",
    )(
        place, send, recv.reshape(1, -1), b_edge.reshape(1, -1), recv_rows, lat, lat_p2, w_ep, w_p3, *shards
    )


def on_device(
    grid_in,
    g2m_geom,
    g2m_src,
    g2m_dst,
    g2m_node,
    mesh_emb,
    mesh_send,
    mesh_recv,
    w_in1,
    b_in,
    w_in2,
    w_g2m,
    w_geo,
    b_g2m,
    w_enc1,
    b_enc,
    w_enc2,
    w_snd,
    w_rcv,
    b_edge,
    w_edge,
    w_p1,
    w_p2,
    b_p,
    w_p3,
):
    groups, places = lax.axis_size("grp"), lax.axis_size("inner")
    bands = groups * places
    nodes_here = mesh_emb.shape[0]
    band = lax.axis_index(BOTH)
    place = lax.axis_index("inner")
    core = place % 2

    def by_parity(even, odd):
        pairs = [(b, b + (odd if b % 2 else even)) for b in range(bands)]
        pairs = [pair for pair in pairs if 0 <= pair[1] < bands]
        return lambda value: lax.ppermute(value, BOTH, pairs)

    def onward(value):
        pairs = [(i, (i + (-2 if i % 2 else 2)) % places) for i in range(places)]
        return lax.ppermute(value, "inner", pairs)

    def across(value):
        return lax.ppermute(value, "inner", [(i, (i + 4) % places) for i in range(places)])

    def along_groups(value, by):
        pairs = [(i, i + by) for i in range(groups) if 0 <= i + by < groups]
        return lax.ppermute(value, "grp", pairs)

    other_core = by_parity(1, -1)

    turn = 1 - 2 * core
    scalars = jnp.stack([band, turn, jnp.int32(nodes_here)])
    back2, back1, own, on1, on2 = band_sums(
        scalars,
        nodes_here,
        g2m_src,
        grid_in.T,
        w_in1,
        b_in.reshape(1, -1),
        w_in2,
        w_g2m,
        g2m_geom,
        w_geo,
        b_g2m.reshape(1, -1),
        g2m_dst.reshape(1, -1),
        g2m_node.reshape(1, -1),
    )
    crossing = other_core(back1)
    two = by_parity(-2, 2)(back2)
    one = by_parity(2, -2)((on2 + crossing.astype(F32)).astype(BF16))
    near = other_core(on1)
    mesh_lat, senders = encoder(own, near, one, two, mesh_emb, w_enc1, b_enc, w_enc2, w_snd)

    partner = other_core(senders)
    next_a = onward(senders)
    far = across(senders)
    next_b = onward(partner)
    low = along_groups(senders, 1)
    high = along_groups(senders, -1)
    shards = [senders, partner, next_a, next_b, far]
    shards = shards + [other_core(shard) for shard in shards[2:]] + [low, high]
    recv_rows, w_ep, lat_p2 = receiver_side(mesh_recv, mesh_lat, w_rcv, w_edge, w_p1, w_p2, b_p)
    before, after, opposite = [(place + by) % places for by in (-2 * turn, 2 * turn, 4)]
    where = [place, place + turn, before, before + turn, opposite]
    where = where + [after + turn, after, opposite + turn, places, places + 1]
    starts = jnp.stack([jnp.asarray(p, jnp.int32) for p in where]) * nodes_here
    return processor(
        starts, mesh_send, mesh_recv, b_edge, recv_rows, mesh_lat, lat_p2, w_ep, w_p3, shards
    )


def solution(mesh):
    split = P(BOTH)
    rows = P(BOTH, None)
    return jax.shard_map(
        on_device,
        mesh=mesh,
        in_specs=(rows, P(None, BOTH), split, rows, split, rows, split, split) + (P(),) * 17,
        out_specs=rows,
        check_vma=False,
    )
```

```python
import jax
import jax.numpy as jnp
from jax import lax
from jax.experimental import pallas as pl
from jax.experimental.pallas import tpu as pltpu
from jax.sharding import PartitionSpec as P

F32 = jnp.float32
BF16 = jnp.bfloat16
LANES = 128
EDGE_BLOCK = 256
BOTH = ("grp", "inner")
MESSAGE_VMEM = 57 * 2**20
PROCESSOR_VMEM = 40 * 2**20


def silu(v):
    half = v * 0.5
    return half + half * jnp.tanh(half)


def split3(v):
    high = v.astype(BF16).astype(F32)
    rest = v - high
    mid = rest.astype(BF16).astype(F32)
    return high, mid, (rest - mid).astype(BF16).astype(F32)


def dot(a, b):
    return jnp.dot(a, b, preferred_element_type=F32)


def dot_first(a, b):
    return lax.dot_general(a, b, (((0,), (0,)), ((), ())), preferred_element_type=F32)


def one_hot(ids, rows):
    numbers = lax.broadcasted_iota(jnp.int32, (rows, ids.shape[1]), 0)
    return jnp.where(numbers == ids, 1.0, 0.0).astype(BF16)


def put_rows(table, first, rows):
    parts = rows.shape[1] // LANES
    for j in range(parts):
        table[pl.ds(first * parts + j, rows.shape[0], stride=parts), :] = rows[
            :, j * LANES : (j + 1) * LANES
        ]


def message_kernel(
    src_hbm, grid_hbm, w_in1_hbm, b_in_hbm, w_in2_hbm, w_g2m_hbm, geom_hbm, w_geo_hbm, b_g2m_hbm, dst_hbm, node_hbm,
    back2, back1, own, on1, on2,
    src_rows, grid_in, w_in1, b_in, w_in2, w_g2m, geom, w_geo, b_g2m, dst, node, src, table, buf_a, buf_b, w8, g8, w48, w_both, msg_a, msg_b, sums, sems,
):
    nodes, edges = grid_in.shape[1], src.shape[0]
    places = lax.axis_size("inner")
    place = lax.axis_index("inner")
    band = lax.axis_index("grp") * places + place
    turn = 1 - 2 * lax.rem(place, 2)
    bands, rows = 5, own.shape[0]
    chunk = 512
    chunks = nodes // chunk
    here = [
        (w_in1_hbm, w_in1), (b_in_hbm, b_in), (w_in2_hbm, w_in2), (w_g2m_hbm, w_g2m), (src_hbm, src_rows),
        (geom_hbm, geom), (w_geo_hbm, w_geo), (b_g2m_hbm, b_g2m), (dst_hbm, dst), (node_hbm, node),
    ]
    copies = [pltpu.make_async_copy(a, b, sems.at[i]) for i, (a, b) in enumerate(here)]
    grids = []
    for k in range(chunks):
        part = pl.ds(k * chunk, chunk)
        grids.append(
            pltpu.make_async_copy(grid_hbm.at[:, part], grid_in.at[:, part], sems.at[len(here) + k])
        )
    for copy in [copies[0], grids[0], copies[1], copies[4], copies[2], copies[3]] + grids[1:] + copies[5:]:
        copy.start()
    copies[4].wait()
    src_rows[...] = src_rows[...] * 4
    to_scalars = pltpu.make_async_copy(src_rows.at[0], src, sems.at[len(here) + chunks])
    to_scalars.start()
    copies[0].wait()
    copies[1].wait()
    for k in range(chunks):
        grids[k].wait()
        hid = dot_first(grid_in[:, k * chunk : (k + 1) * chunk], w_in1[...])
        hid = silu(hid + b_in[...]).astype(BF16)
        if k == 0:
            copies[2].wait()
            copies[3].wait()
            w_both[...] = dot(w_in2[...], w_g2m[...]).astype(BF16)
        put_rows(table, k * chunk, dot(hid, w_both[...]))

    to_scalars.wait()
    for copy in copies[5:]:
        copy.wait()
    node[...] = ((dst[...] - band) * turn + 2) * rows + node[...]
    w8[...] = jnp.zeros_like(w8)
    w8[0:4, :] = w_geo[...]
    w8[4:5, :] = b_g2m[...]
    high, mid, low = split3(w8[...])
    w48[...] = jnp.concatenate([high, high, high, mid, mid, low], axis=0).astype(BF16)
    g8[...] = jnp.zeros_like(g8)
    g8[0:4, :] = geom[...]
    g8[4:5, :] = jnp.ones((1, g8.shape[1]), F32)
    sums[...] = jnp.zeros_like(sums)
    msg_b[...] = jnp.zeros_like(msg_b)

    def gather(base, buf):
        for e in range(EDGE_BLOCK):
            row = pl.multiple_of(src[base + e], 4)
            buf[4 * e : 4 * e + 4, :] = table[pl.ds(row, 4), :]

    def emit(base, half, buf):
        base = pl.multiple_of(base, EDGE_BLOCK)
        high, mid, low = split3(g8[:, pl.ds(base, EDGE_BLOCK)])
        g48 = jnp.concatenate([high, mid, low, high, mid, high], axis=0).astype(BF16)
        geo = dot_first(g48, w48[...])
        for j in range(4):
            lanes = slice(j * LANES, (j + 1) * LANES)
            v = buf[pl.ds(j, EDGE_BLOCK, stride=4), :] + geo[:, lanes]
            (msg_a, msg_b)[half][:, lanes] = silu(v).astype(BF16)

    def scatter(base, half):
        base = pl.multiple_of(jnp.maximum(base, 0), EDGE_BLOCK)
        select = one_hot(node[:, pl.ds(base, EDGE_BLOCK)], bands * rows)
        sums[...] += dot(select, (msg_a, msg_b)[half][...])

    blocks = edges // EDGE_BLOCK
    gather(0, buf_a)

    def step(t, carry):
        base = pl.multiple_of(t * (2 * EDGE_BLOCK), 2 * EDGE_BLOCK)
        gather(base + EDGE_BLOCK, buf_b)
        emit(base, 0, buf_a)
        scatter(base - EDGE_BLOCK, 1)
        gather(jnp.minimum(base + 2 * EDGE_BLOCK, (blocks - 1) * EDGE_BLOCK), buf_a)
        emit(base + EDGE_BLOCK, 1, buf_b)
        scatter(base, 0)
        return carry

    lax.fori_loop(0, blocks // 2, step, 0)
    scatter(edges - EDGE_BLOCK, 1)
    for which, out in enumerate((back2, back1, own, on1, on2)):
        out[...] = sums[which * rows : (which + 1) * rows, :].astype(out.dtype)


def band_sums(rows, *arrays):
    g2m_src, grid_in, w_in1 = arrays[:3]
    edges, nodes, width = g2m_src.shape[1], grid_in.shape[1], w_in1.shape[1]
    vmem = pl.BlockSpec(memory_space=pltpu.VMEM)
    hbm = pl.BlockSpec(memory_space=pltpu.HBM)
    return pl.pallas_call(
        message_kernel,
        out_shape=[jax.ShapeDtypeStruct((rows, width), dtype) for dtype in [BF16] * 5],
        in_specs=[hbm] * len(arrays),
        out_specs=[vmem] * 5,
        scratch_shapes=[pltpu.VMEM(a.shape, a.dtype) for a in arrays]
        + [
            pltpu.SMEM((edges,), jnp.int32),
            pltpu.VMEM((4 * nodes, LANES), F32),
            pltpu.VMEM((4 * EDGE_BLOCK, LANES), F32),
            pltpu.VMEM((4 * EDGE_BLOCK, LANES), F32),
            pltpu.VMEM((8, width), F32),
            pltpu.VMEM((8, edges), F32),
            pltpu.VMEM((48, width), BF16),
            pltpu.VMEM((width, width), BF16),
            pltpu.VMEM((EDGE_BLOCK, width), BF16),
            pltpu.VMEM((EDGE_BLOCK, width), BF16),
            pltpu.VMEM((5 * rows, width), F32),
            pltpu.SemaphoreType.DMA((len(arrays) + 4,)),
        ],
        compiler_params=pltpu.CompilerParams(vmem_limit_bytes=MESSAGE_VMEM),
        name="band_sums",
    )(*arrays)


def encoder_kernel(some, one, emb, w_enc1, b_enc, w_enc2, w_snd, lat, snd):
    total = some[...].astype(F32) + one[...].astype(F32)
    enc = silu(dot(total.astype(BF16), w_enc1[...]) + b_enc[...]).astype(BF16)
    mesh_lat = (emb[...].astype(F32) + dot(enc, w_enc2[...])).astype(BF16)
    lat[...] = mesh_lat
    snd[...] = dot(mesh_lat, w_snd[...]).astype(BF16)


def encoder(some, one, emb, w_enc1, b_enc, w_enc2, w_snd):
    vmem = pl.BlockSpec(memory_space=pltpu.VMEM)
    rows, width = emb.shape
    return pl.pallas_call(
        encoder_kernel,
        out_shape=[jax.ShapeDtypeStruct((rows, width), BF16)] * 2,
        in_specs=[vmem] * 7,
        out_specs=[vmem] * 2,
        compiler_params=pltpu.CompilerParams(vmem_limit_bytes=16 * 2**20),
        name="encoder",
    )(some, one, emb, w_enc1, b_enc.reshape(1, -1), w_enc2, w_snd)


def receiver_kernel(send, lat, w_rcv, w_edge, w_p1, w_p2, b_p, b_edge, w_p3, packed, packed32, offsets):
    offsets[...] = send[...] * 4
    rows, width = lat.shape
    packed[0:width, :] = dot(w_edge[...], w_p1[...]).astype(BF16)
    packed[width : 2 * width, :] = w_p3[...]
    packed[2 * width : 2 * width + rows, :] = lat[...]
    packed32[0:rows, :] = dot(lat[...], w_p2[...]) + b_p[...]
    packed32[rows : rows + 8, :] = jnp.broadcast_to(b_edge[...], (8, width))
    packed[2 * width + rows :, :] = dot(lat[...], w_rcv[...]).astype(BF16)


def receiver_side(send, lat, w_rcv, w_edge, w_p1, w_p2, b_p, b_edge, w_p3):
    vmem = pl.BlockSpec(memory_space=pltpu.VMEM)
    rows, width = lat.shape
    edges = send.shape[0]
    return pl.pallas_call(
        receiver_kernel,
        out_shape=[
            jax.ShapeDtypeStruct((2 * width + 2 * rows, width), BF16),
            jax.ShapeDtypeStruct((rows + 8, width), F32),
            jax.ShapeDtypeStruct((1, edges), jnp.int32),
        ],
        in_specs=[vmem] * 9,
        out_specs=[vmem] * 3,
        compiler_params=pltpu.CompilerParams(vmem_limit_bytes=12 * 2**20),
        cost_estimate=pl.CostEstimate(flops=10**9, bytes_accessed=6 * 10**6, transcendentals=0),
        name="receiver_side",
    )(
        send.reshape(1, -1), lat, w_rcv, w_edge, w_p1, w_p2,
        b_p.reshape(1, -1), b_edge.reshape(1, -1), w_p3,
    )


def processor_kernel(place, send, recv, packed_hbm, packed32_hbm, *refs):
    count = 10
    out, packed, packed32, shard, table, buf_a, buf_b, hid_a, hid_b, agg, sems = refs[count:]
    rows, width = out.shape
    shards = refs[:count]
    copies = [pltpu.make_async_copy(shards[k], shard.at[k], sems.at[k]) for k in range(count)]
    copies.append(pltpu.make_async_copy(packed32_hbm, packed32, sems.at[count]))
    copies.append(pltpu.make_async_copy(packed_hbm, packed, sems.at[count + 1]))
    for copy in copies:
        copy.start()
    lat = packed.at[2 * width : 2 * width + rows]
    receivers = packed.at[2 * width + rows : 2 * width + 2 * rows]
    agg[...] = jnp.zeros_like(agg)
    hid_b[...] = jnp.zeros_like(hid_b)
    for k in range(count):
        copies[k].wait()
        put_rows(table, place[k], shard[k].astype(F32))
    copies[count].wait()
    copies[count + 1].wait()

    def gather(base, buf):
        for e in range(EDGE_BLOCK):
            row = pl.multiple_of(send[0, base + e], 4)
            buf[4 * e : 4 * e + 4, :] = table[pl.ds(row, 4), :]

    def select(base):
        base = pl.multiple_of(base, EDGE_BLOCK)
        return one_hot(recv[:, pl.ds(base, EDGE_BLOCK)], rows)

    def emit(base, buf, hid):
        received = dot_first(select(base), receivers[...]) + packed32[rows : rows + 1, :]
        for j in range(4):
            lanes = slice(j * LANES, (j + 1) * LANES)
            v = buf[pl.ds(j, EDGE_BLOCK, stride=4), :] + received[:, lanes]
            hid[:, lanes] = silu(v).astype(BF16)

    def add_up(base, hid):
        agg[...] += dot(select(jnp.maximum(base, 0)), hid[...])

    blocks = send.shape[1] // EDGE_BLOCK
    gather(0, buf_a)

    def step(t, carry):
        base = t * (2 * EDGE_BLOCK)
        gather(base + EDGE_BLOCK, buf_b)
        emit(base, buf_a, hid_a)
        add_up(base - EDGE_BLOCK, hid_b)
        gather(jnp.minimum(base + 2 * EDGE_BLOCK, (blocks - 1) * EDGE_BLOCK), buf_a)
        emit(base + EDGE_BLOCK, buf_b, hid_b)
        add_up(base, hid_a)
        return carry

    lax.fori_loop(0, blocks // 2, step, 0)
    add_up((blocks - 1) * EDGE_BLOCK, hid_b)
    node = dot(agg[...].astype(BF16), packed[0:width, :]) + packed32[0:rows, :]
    change = dot(silu(node).astype(BF16), packed[width : 2 * width, :])
    out[...] = (lat[...].astype(F32) + change).astype(BF16)


def processor(place, send, recv, packed, packed32, shards):
    vmem = pl.BlockSpec(memory_space=pltpu.VMEM)
    smem = pl.BlockSpec(memory_space=pltpu.SMEM)
    hbm = pl.BlockSpec(memory_space=pltpu.HBM)
    rows, width = shards[0].shape
    return pl.pallas_call(
        processor_kernel,
        out_shape=jax.ShapeDtypeStruct((rows, width), BF16),
        in_specs=[smem, smem, vmem] + [hbm] * (2 + len(shards)),
        out_specs=vmem,
        scratch_shapes=[
            pltpu.VMEM(packed.shape, BF16),
            pltpu.VMEM(packed32.shape, F32),
            pltpu.VMEM((len(shards), rows, width), BF16),
            pltpu.VMEM((4 * len(shards) * rows, LANES), F32),
            pltpu.VMEM((4 * EDGE_BLOCK, LANES), F32),
            pltpu.VMEM((4 * EDGE_BLOCK, LANES), F32),
            pltpu.VMEM((EDGE_BLOCK, width), BF16),
            pltpu.VMEM((EDGE_BLOCK, width), BF16),
            pltpu.VMEM((rows, width), F32),
            pltpu.SemaphoreType.DMA((len(shards) + 2,)),
        ],
        compiler_params=pltpu.CompilerParams(vmem_limit_bytes=PROCESSOR_VMEM),
        name="processor",
    )(place, send, recv.reshape(1, -1), packed, packed32, *shards)


def on_device(
    grid_in,
    g2m_geom,
    g2m_src,
    g2m_dst,
    g2m_node,
    mesh_emb,
    mesh_send,
    mesh_recv,
    w_in1,
    b_in,
    w_in2,
    w_g2m,
    w_geo,
    b_g2m,
    w_enc1,
    b_enc,
    w_enc2,
    w_snd,
    w_rcv,
    b_edge,
    w_edge,
    w_p1,
    w_p2,
    b_p,
    w_p3,
):
    groups, places = lax.axis_size("grp"), lax.axis_size("inner")
    bands = groups * places
    nodes_here = mesh_emb.shape[0]
    place = lax.axis_index("inner")
    core = place % 2

    def by_parity(even, odd):
        pairs = [(b, b + (odd if b % 2 else even)) for b in range(bands)]
        pairs = [pair for pair in pairs if 0 <= pair[1] < bands]
        return lambda value: lax.ppermute(value, BOTH, pairs)

    def onward(value):
        pairs = [(i, (i + (-2 if i % 2 else 2)) % places) for i in range(places)]
        return lax.ppermute(value, "inner", pairs)

    def across(value):
        return lax.ppermute(value, "inner", [(i, (i + 4) % places) for i in range(places)])

    def along_groups(value, by):
        pairs = [(i, i + by) for i in range(groups) if 0 <= i + by < groups]
        return lax.ppermute(value, "grp", pairs)

    other_core = by_parity(1, -1)

    turn = 1 - 2 * core
    back2, back1, own, on1, on2 = band_sums(
        nodes_here,
        g2m_src.reshape(1, -1),
        grid_in.T,
        w_in1,
        b_in.reshape(1, -1),
        w_in2,
        w_g2m,
        g2m_geom,
        w_geo,
        b_g2m.reshape(1, -1),
        g2m_dst.reshape(1, -1),
        g2m_node.reshape(1, -1),
    )
    crossing = other_core(back1)
    two = by_parity(-2, 2)(back2)
    joint = (on2.astype(F32) + crossing.astype(F32)).astype(BF16)
    one = by_parity(2, -2)(joint)
    on1, _ = lax.optimization_barrier((on1, joint))
    near = other_core(on1)
    some = own.astype(F32) + near.astype(F32) + two.astype(F32)
    mesh_lat, senders = encoder(some.astype(BF16), one, mesh_emb, w_enc1, b_enc, w_enc2, w_snd)

    partner = other_core(senders)
    next_a = onward(senders)
    far = across(senders)
    next_b = onward(partner)
    low = along_groups(senders, 1)
    high = along_groups(senders, -1)
    packed, packed32, offsets = receiver_side(
        mesh_send, mesh_lat, w_rcv, w_edge, w_p1, w_p2, b_p, b_edge, w_p3
    )
    next_a, offsets = lax.optimization_barrier((next_a, offsets))
    shards = [senders, partner, next_a, next_b, far]
    shards = shards + [other_core(shard) for shard in shards[2:]] + [low, high]
    before, after, opposite = [(place + by) % places for by in (-2 * turn, 2 * turn, 4)]
    where = [place, place + turn, before, before + turn, opposite]
    where = where + [after + turn, after, opposite + turn, places, places + 1]
    starts = jnp.stack([jnp.asarray(p, jnp.int32) for p in where]) * nodes_here
    return processor(starts, offsets, mesh_recv, packed, packed32, shards)


def solution(mesh):
    split = P(BOTH)
    rows = P(BOTH, None)
    return jax.shard_map(
        on_device,
        mesh=mesh,
        in_specs=(rows, P(None, BOTH), split, rows, split, rows, split, split) + (P(),) * 17,
        out_specs=rows,
        check_vma=False,
    )
```

```python
import jax
import jax.numpy as jnp
from jax import lax
from jax.experimental import pallas as pl
from jax.experimental.pallas import tpu as pltpu
from jax.sharding import PartitionSpec as P

F32 = jnp.float32
BF16 = jnp.bfloat16
LANES = 128
EDGE_BLOCK = 256
BOTH = ("grp", "inner")
MESSAGE_VMEM = 57 * 2**20
PROCESSOR_VMEM = 40 * 2**20
NEAR_SHARDS = 3


def silu(v):
    half = v * 0.5
    return half + half * jnp.tanh(half)


def split3(v):
    high = v.astype(BF16).astype(F32)
    rest = v - high
    mid = rest.astype(BF16).astype(F32)
    return high, mid, (rest - mid).astype(BF16).astype(F32)


def dot(a, b):
    return jnp.dot(a, b, preferred_element_type=F32)


def dot_first(a, b):
    return lax.dot_general(a, b, (((0,), (0,)), ((), ())), preferred_element_type=F32)


def one_hot(ids, rows):
    numbers = lax.broadcasted_iota(jnp.int32, (rows, ids.shape[1]), 0)
    return jnp.where(numbers == ids, 1.0, 0.0).astype(BF16)


def put_rows(table, first, rows):
    parts = rows.shape[1] // LANES
    for j in range(parts):
        table[pl.ds(first * parts + j, rows.shape[0], stride=parts), :] = rows[
            :, j * LANES : (j + 1) * LANES
        ]


def message_kernel(
    src_hbm, grid_hbm, w_in1_hbm, b_in_hbm, w_in2_hbm, w_g2m_hbm, geom_hbm, w_geo_hbm, b_g2m_hbm, dst_hbm, node_hbm,
    back2, back1, own, on1, on2,
    src_rows, grid_in, w_in1, b_in, w_in2, w_g2m, geom, w_geo, b_g2m, dst, node, src, table, buf_a, buf_b, w8, g8, w48, w_both, msg_a, msg_b, sums, sems,
):
    nodes, edges = grid_in.shape[1], src.shape[0]
    places = lax.axis_size("inner")
    place = lax.axis_index("inner")
    band = lax.axis_index("grp") * places + place
    turn = 1 - 2 * lax.rem(place, 2)
    bands, rows = 5, own.shape[0]
    chunk = 1024
    chunks = nodes // chunk
    here = [
        (w_in1_hbm, w_in1), (b_in_hbm, b_in), (w_in2_hbm, w_in2), (w_g2m_hbm, w_g2m), (src_hbm, src_rows),
        (geom_hbm, geom), (w_geo_hbm, w_geo), (b_g2m_hbm, b_g2m), (dst_hbm, dst), (node_hbm, node),
    ]
    copies = [pltpu.make_async_copy(a, b, sems.at[i]) for i, (a, b) in enumerate(here)]
    grids = []
    for k in range(chunks):
        part = pl.ds(k * chunk, chunk)
        grids.append(
            pltpu.make_async_copy(grid_hbm.at[:, part], grid_in.at[:, part], sems.at[len(here) + k])
        )
    for copy in [copies[0], grids[0], copies[1], copies[4], copies[2], copies[3]] + grids[1:] + copies[5:]:
        copy.start()
    copies[4].wait()
    src_rows[...] = src_rows[...] * 4
    to_scalars = pltpu.make_async_copy(src_rows.at[0], src, sems.at[len(here) + chunks])
    to_scalars.start()
    copies[0].wait()
    copies[1].wait()
    for k in range(chunks):
        grids[k].wait()
        hid = dot_first(grid_in[:, k * chunk : (k + 1) * chunk], w_in1[...])
        hid = silu(hid + b_in[...]).astype(BF16)
        if k == 0:
            copies[2].wait()
            copies[3].wait()
            w_both[...] = dot(w_in2[...], w_g2m[...]).astype(BF16)
        put_rows(table, k * chunk, dot(hid, w_both[...]))

    to_scalars.wait()
    for copy in copies[5:]:
        copy.wait()
    node[...] = ((dst[...] - band) * turn + 2) * rows + node[...]
    w8[...] = jnp.zeros_like(w8)
    w8[0:4, :] = w_geo[...]
    w8[4:5, :] = b_g2m[...]
    high, mid, low = split3(w8[...])
    w48[...] = jnp.concatenate([high, high, high, mid, mid, low], axis=0).astype(BF16)
    g8[...] = jnp.zeros_like(g8)
    g8[0:4, :] = geom[...]
    g8[4:5, :] = jnp.ones((1, g8.shape[1]), F32)
    sums[...] = jnp.zeros_like(sums)
    msg_b[...] = jnp.zeros_like(msg_b)

    def gather(base, buf):
        for e in range(EDGE_BLOCK):
            row = pl.multiple_of(src[base + e], 4)
            buf[4 * e : 4 * e + 4, :] = table[pl.ds(row, 4), :]

    def emit(base, half, buf):
        base = pl.multiple_of(base, EDGE_BLOCK)
        high, mid, low = split3(g8[:, pl.ds(base, EDGE_BLOCK)])
        g48 = jnp.concatenate([high, mid, low, high, mid, high], axis=0).astype(BF16)
        geo = dot_first(g48, w48[...])
        for j in range(4):
            lanes = slice(j * LANES, (j + 1) * LANES)
            v = buf[pl.ds(j, EDGE_BLOCK, stride=4), :] + geo[:, lanes]
            (msg_a, msg_b)[half][:, lanes] = silu(v).astype(BF16)

    def scatter(base, half):
        base = pl.multiple_of(jnp.maximum(base, 0), EDGE_BLOCK)
        select = one_hot(node[:, pl.ds(base, EDGE_BLOCK)], bands * rows)
        sums[...] += dot(select, (msg_a, msg_b)[half][...])

    blocks = edges // EDGE_BLOCK
    gather(0, buf_a)

    def step(t, carry):
        base = pl.multiple_of(t * (2 * EDGE_BLOCK), 2 * EDGE_BLOCK)
        gather(base + EDGE_BLOCK, buf_b)
        emit(base, 0, buf_a)
        scatter(base - EDGE_BLOCK, 1)
        gather(jnp.minimum(base + 2 * EDGE_BLOCK, (blocks - 1) * EDGE_BLOCK), buf_a)
        emit(base + EDGE_BLOCK, 1, buf_b)
        scatter(base, 0)
        return carry

    lax.fori_loop(0, blocks // 2, step, 0)
    scatter(edges - EDGE_BLOCK, 1)
    for which, out in enumerate((back2, back1, own, on1, on2)):
        out[...] = sums[which * rows : (which + 1) * rows, :].astype(out.dtype)


def band_sums(rows, *arrays):
    g2m_src, grid_in, w_in1 = arrays[:3]
    edges, nodes, width = g2m_src.shape[1], grid_in.shape[1], w_in1.shape[1]
    vmem = pl.BlockSpec(memory_space=pltpu.VMEM)
    hbm = pl.BlockSpec(memory_space=pltpu.HBM)
    return pl.pallas_call(
        message_kernel,
        out_shape=[jax.ShapeDtypeStruct((rows, width), dtype) for dtype in [BF16] * 5],
        in_specs=[hbm] * len(arrays),
        out_specs=[vmem] * 5,
        scratch_shapes=[pltpu.VMEM(a.shape, a.dtype) for a in arrays]
        + [
            pltpu.SMEM((edges,), jnp.int32),
            pltpu.VMEM((4 * nodes, LANES), F32),
            pltpu.VMEM((4 * EDGE_BLOCK, LANES), F32),
            pltpu.VMEM((4 * EDGE_BLOCK, LANES), F32),
            pltpu.VMEM((8, width), F32),
            pltpu.VMEM((8, edges), F32),
            pltpu.VMEM((48, width), BF16),
            pltpu.VMEM((width, width), BF16),
            pltpu.VMEM((EDGE_BLOCK, width), BF16),
            pltpu.VMEM((EDGE_BLOCK, width), BF16),
            pltpu.VMEM((5 * rows, width), F32),
            pltpu.SemaphoreType.DMA((len(arrays) + 4,)),
        ],
        compiler_params=pltpu.CompilerParams(vmem_limit_bytes=MESSAGE_VMEM),
        name="band_sums",
    )(*arrays)


def encoder_kernel(some, one, emb, w_enc1, b_enc, w_enc2, w_snd, lat, snd):
    total = some[...].astype(F32) + one[...].astype(F32)
    enc = silu(dot(total.astype(BF16), w_enc1[...]) + b_enc[...]).astype(BF16)
    mesh_lat = (emb[...].astype(F32) + dot(enc, w_enc2[...])).astype(BF16)
    lat[...] = mesh_lat
    snd[...] = dot(mesh_lat, w_snd[...]).astype(BF16)


def encoder(some, one, emb, w_enc1, b_enc, w_enc2, w_snd):
    vmem = pl.BlockSpec(memory_space=pltpu.VMEM)
    rows, width = emb.shape
    return pl.pallas_call(
        encoder_kernel,
        out_shape=[jax.ShapeDtypeStruct((rows, width), BF16)] * 2,
        in_specs=[vmem] * 7,
        out_specs=[vmem] * 2,
        compiler_params=pltpu.CompilerParams(vmem_limit_bytes=16 * 2**20),
        name="encoder",
    )(some, one, emb, w_enc1, b_enc.reshape(1, -1), w_enc2, w_snd)


def receiver_kernel(send, lat, w_rcv, w_edge, w_p1, w_p2, b_p, b_edge, w_p3, packed, packed32, offsets):
    offsets[...] = send[...] * 4
    rows, width = lat.shape
    packed[0:width, :] = dot(w_edge[...], w_p1[...]).astype(BF16)
    packed[width : 2 * width, :] = w_p3[...]
    packed[2 * width : 2 * width + rows, :] = lat[...]
    packed32[0:rows, :] = dot(lat[...], w_p2[...]) + b_p[...]
    packed32[rows : rows + 8, :] = jnp.broadcast_to(b_edge[...], (8, width))
    packed[2 * width + rows :, :] = dot(lat[...], w_rcv[...]).astype(BF16)


def receiver_side(send, lat, w_rcv, w_edge, w_p1, w_p2, b_p, b_edge, w_p3):
    vmem = pl.BlockSpec(memory_space=pltpu.VMEM)
    rows, width = lat.shape
    edges = send.shape[0]
    return pl.pallas_call(
        receiver_kernel,
        out_shape=[
            jax.ShapeDtypeStruct((2 * width + 2 * rows, width), BF16),
            jax.ShapeDtypeStruct((rows + 8, width), F32),
            jax.ShapeDtypeStruct((1, edges), jnp.int32),
        ],
        in_specs=[vmem] * 9,
        out_specs=[vmem] * 3,
        compiler_params=pltpu.CompilerParams(vmem_limit_bytes=12 * 2**20),
        cost_estimate=pl.CostEstimate(flops=10**9, bytes_accessed=6 * 10**6, transcendentals=0),
        name="receiver_side",
    )(
        send.reshape(1, -1), lat, w_rcv, w_edge, w_p1, w_p2,
        b_p.reshape(1, -1), b_edge.reshape(1, -1), w_p3,
    )


def processor_kernel(place, send, recv, packed, packed32, *refs):
    count, near = 10, NEAR_SHARDS
    out, shard, table, buf_a, buf_b, hid_a, hid_b, agg, sems = refs[count:]
    rows, width = out.shape
    lat = packed.at[2 * width : 2 * width + rows]
    receivers = packed.at[2 * width + rows : 2 * width + 2 * rows]
    copies = []
    for k in range(near, count):
        copies.append(pltpu.make_async_copy(refs[k], shard.at[k - near], sems.at[k - near]))
        copies[-1].start()
    agg[...] = jnp.zeros_like(agg)
    hid_b[...] = jnp.zeros_like(hid_b)
    for k in range(near):
        put_rows(table, place[k], refs[k][...].astype(F32))
    for k in range(near, count):
        copies[k - near].wait()
        put_rows(table, place[k], shard[k - near].astype(F32))

    def gather(base, buf):
        for e in range(EDGE_BLOCK):
            row = pl.multiple_of(send[0, base + e], 4)
            buf[4 * e : 4 * e + 4, :] = table[pl.ds(row, 4), :]

    def select(base):
        base = pl.multiple_of(base, EDGE_BLOCK)
        return one_hot(recv[:, pl.ds(base, EDGE_BLOCK)], rows)

    def emit(base, buf, hid):
        received = dot_first(select(base), receivers[...]) + packed32[rows : rows + 1, :]
        for j in range(4):
            lanes = slice(j * LANES, (j + 1) * LANES)
            v = buf[pl.ds(j, EDGE_BLOCK, stride=4), :] + received[:, lanes]
            hid[:, lanes] = silu(v).astype(BF16)

    def add_up(base, hid):
        agg[...] += dot(select(jnp.maximum(base, 0)), hid[...])

    blocks = send.shape[1] // EDGE_BLOCK
    gather(0, buf_a)

    def step(t, carry):
        base = t * (2 * EDGE_BLOCK)
        gather(base + EDGE_BLOCK, buf_b)
        emit(base, buf_a, hid_a)
        add_up(base - EDGE_BLOCK, hid_b)
        gather(jnp.minimum(base + 2 * EDGE_BLOCK, (blocks - 1) * EDGE_BLOCK), buf_a)
        emit(base + EDGE_BLOCK, buf_b, hid_b)
        add_up(base, hid_a)
        return carry

    lax.fori_loop(0, blocks // 2, step, 0)
    add_up((blocks - 1) * EDGE_BLOCK, hid_b)
    node = dot(agg[...].astype(BF16), packed[0:width, :]) + packed32[0:rows, :]
    change = dot(silu(node).astype(BF16), packed[width : 2 * width, :])
    out[...] = (lat[...].astype(F32) + change).astype(BF16)


def processor(place, send, recv, packed, packed32, shards):
    vmem = pl.BlockSpec(memory_space=pltpu.VMEM)
    smem = pl.BlockSpec(memory_space=pltpu.SMEM)
    hbm = pl.BlockSpec(memory_space=pltpu.HBM)
    rows, width = shards[0].shape
    return pl.pallas_call(
        processor_kernel,
        out_shape=jax.ShapeDtypeStruct((rows, width), BF16),
        in_specs=[smem, smem] + [vmem] * (3 + NEAR_SHARDS) + [hbm] * (len(shards) - NEAR_SHARDS),
        out_specs=vmem,
        scratch_shapes=[
            pltpu.VMEM((len(shards) - NEAR_SHARDS, rows, width), BF16),
            pltpu.VMEM((4 * len(shards) * rows, LANES), F32),
            pltpu.VMEM((4 * EDGE_BLOCK, LANES), F32),
            pltpu.VMEM((4 * EDGE_BLOCK, LANES), F32),
            pltpu.VMEM((EDGE_BLOCK, width), BF16),
            pltpu.VMEM((EDGE_BLOCK, width), BF16),
            pltpu.VMEM((rows, width), F32),
            pltpu.SemaphoreType.DMA((len(shards) - NEAR_SHARDS,)),
        ],
        compiler_params=pltpu.CompilerParams(vmem_limit_bytes=PROCESSOR_VMEM),
        name="processor",
    )(place, send, recv.reshape(1, -1), packed, packed32, *shards)


def on_device(
    grid_in,
    g2m_geom,
    g2m_src,
    g2m_dst,
    g2m_node,
    mesh_emb,
    mesh_send,
    mesh_recv,
    w_in1,
    b_in,
    w_in2,
    w_g2m,
    w_geo,
    b_g2m,
    w_enc1,
    b_enc,
    w_enc2,
    w_snd,
    w_rcv,
    b_edge,
    w_edge,
    w_p1,
    w_p2,
    b_p,
    w_p3,
):
    groups, places = lax.axis_size("grp"), lax.axis_size("inner")
    bands = groups * places
    nodes_here = mesh_emb.shape[0]
    place = lax.axis_index("inner")
    core = place % 2

    def by_parity(even, odd):
        pairs = [(b, b + (odd if b % 2 else even)) for b in range(bands)]
        pairs = [pair for pair in pairs if 0 <= pair[1] < bands]
        return lambda value: lax.ppermute(value, BOTH, pairs)

    def onward(value):
        pairs = [(i, (i + (-2 if i % 2 else 2)) % places) for i in range(places)]
        return lax.ppermute(value, "inner", pairs)

    def across(value):
        return lax.ppermute(value, "inner", [(i, (i + 4) % places) for i in range(places)])

    def along_groups(value, by):
        pairs = [(i, i + by) for i in range(groups) if 0 <= i + by < groups]
        return lax.ppermute(value, "grp", pairs)

    other_core = by_parity(1, -1)

    turn = 1 - 2 * core
    back2, back1, own, on1, on2 = band_sums(
        nodes_here,
        g2m_src.reshape(1, -1),
        grid_in.T,
        w_in1,
        b_in.reshape(1, -1),
        w_in2,
        w_g2m,
        g2m_geom,
        w_geo,
        b_g2m.reshape(1, -1),
        g2m_dst.reshape(1, -1),
        g2m_node.reshape(1, -1),
    )
    crossing = other_core(back1)
    two = by_parity(-2, 2)(back2)
    joint = (on2.astype(F32) + crossing.astype(F32)).astype(BF16)
    one = by_parity(2, -2)(joint)
    on1, _ = lax.optimization_barrier((on1, joint))
    near = other_core(on1)
    some = own.astype(F32) + near.astype(F32) + two.astype(F32)
    mesh_lat, senders = encoder(some.astype(BF16), one, mesh_emb, w_enc1, b_enc, w_enc2, w_snd)

    partner = other_core(senders)
    next_a = onward(senders)
    far = across(senders)
    next_b = onward(partner)
    low = along_groups(senders, 1)
    high = along_groups(senders, -1)
    packed, packed32, offsets = receiver_side(
        mesh_send, mesh_lat, w_rcv, w_edge, w_p1, w_p2, b_p, b_edge, w_p3
    )
    next_a, offsets = lax.optimization_barrier((next_a, offsets))
    shards = [senders, partner, next_a, next_b, far]
    shards = shards + [other_core(shard) for shard in shards[2:]] + [low, high]
    before, after, opposite = [(place + by) % places for by in (-2 * turn, 2 * turn, 4)]
    where = [place, place + turn, before, before + turn, opposite]
    where = where + [after + turn, after, opposite + turn, places, places + 1]
    starts = jnp.stack([jnp.asarray(p, jnp.int32) for p in where]) * nodes_here
    return processor(starts, offsets, mesh_recv, packed, packed32, shards)


def solution(mesh):
    split = P(BOTH)
    rows = P(BOTH, None)
    return jax.shard_map(
        on_device,
        mesh=mesh,
        in_specs=(rows, P(None, BOTH), split, rows, split, rows, split, split) + (P(),) * 17,
        out_specs=rows,
        check_vma=False,
    )
```

```python
import jax
import jax.numpy as jnp
from jax import lax
from jax.experimental import pallas as pl
from jax.experimental.pallas import tpu as pltpu
from jax.sharding import PartitionSpec as P

F32 = jnp.float32
BF16 = jnp.bfloat16
LANES = 128
EDGE_BLOCK = 256
BOTH = ("grp", "inner")
MESSAGE_VMEM = 57 * 2**20
PROCESSOR_VMEM = 40 * 2**20
NEAR_SHARDS = 3


def silu(v):
    half = v * 0.5
    return half + half * jnp.tanh(half)


def split3(v):
    high = v.astype(BF16).astype(F32)
    rest = v - high
    mid = rest.astype(BF16).astype(F32)
    return high, mid, (rest - mid).astype(BF16).astype(F32)


def dot(a, b):
    return jnp.dot(a, b, preferred_element_type=F32)


def dot_first(a, b):
    return lax.dot_general(a, b, (((0,), (0,)), ((), ())), preferred_element_type=F32)


def one_hot(ids, rows):
    numbers = lax.broadcasted_iota(jnp.int32, (rows, ids.shape[1]), 0)
    return jnp.where(numbers == ids, 1.0, 0.0).astype(BF16)


def put_rows(table, first, rows):
    parts = rows.shape[1] // LANES
    for j in range(parts):
        table[pl.ds(first * parts + j, rows.shape[0], stride=parts), :] = rows[
            :, j * LANES : (j + 1) * LANES
        ]


def message_kernel(
    src_hbm, grid_hbm, w_in1_hbm, b_in_hbm, w_in2_hbm, w_g2m_hbm, geom_hbm, w_geo_hbm, b_g2m_hbm, dst_hbm, node_hbm,
    back2, back1, own, on1, on2,
    src_rows, grid_in, w_in1, b_in, w_in2, w_g2m, geom, w_geo, b_g2m, dst, node, src, table, buf_a, buf_b, w8, g8, w48, w_both, msg_a, msg_b, sums, sems,
):
    nodes, edges = grid_in.shape[1], src.shape[0]
    places = lax.axis_size("inner")
    place = lax.axis_index("inner")
    band = lax.axis_index("grp") * places + place
    turn = 1 - 2 * lax.rem(place, 2)
    bands, rows = 5, own.shape[0]
    chunk = 1024
    chunks = nodes // chunk
    here = [
        (w_in1_hbm, w_in1), (b_in_hbm, b_in), (w_in2_hbm, w_in2), (w_g2m_hbm, w_g2m), (src_hbm, src_rows),
        (geom_hbm, geom), (w_geo_hbm, w_geo), (b_g2m_hbm, b_g2m), (dst_hbm, dst), (node_hbm, node),
    ]
    copies = [pltpu.make_async_copy(a, b, sems.at[i]) for i, (a, b) in enumerate(here)]
    grids = []
    for k in range(chunks):
        part = pl.ds(k * chunk, chunk)
        grids.append(
            pltpu.make_async_copy(grid_hbm.at[:, part], grid_in.at[:, part], sems.at[len(here) + k])
        )
    for copy in [copies[0], grids[0], copies[1], copies[4], copies[2], copies[3]] + grids[1:] + copies[5:]:
        copy.start()
    copies[4].wait()
    src_rows[...] = src_rows[...] * 4
    to_scalars = pltpu.make_async_copy(src_rows.at[0], src, sems.at[len(here) + chunks])
    to_scalars.start()
    copies[0].wait()
    copies[1].wait()
    for k in range(chunks):
        grids[k].wait()
        hid = dot_first(grid_in[:, k * chunk : (k + 1) * chunk], w_in1[...])
        hid = silu(hid + b_in[...]).astype(BF16)
        if k == 0:
            copies[2].wait()
            copies[3].wait()
            w_both[...] = dot(w_in2[...], w_g2m[...]).astype(BF16)
        put_rows(table, k * chunk, dot(hid, w_both[...]))

    to_scalars.wait()
    for copy in copies[5:]:
        copy.wait()
    node[...] = ((dst[...] - band) * turn + 2) * rows + node[...]
    w8[...] = jnp.zeros_like(w8)
    w8[0:4, :] = w_geo[...]
    w8[4:5, :] = b_g2m[...]
    high, mid, low = split3(w8[...])
    w48[...] = jnp.concatenate([high, high, high, mid, mid, low], axis=0).astype(BF16)
    g8[...] = jnp.zeros_like(g8)
    g8[0:4, :] = geom[...]
    g8[4:5, :] = jnp.ones((1, g8.shape[1]), F32)
    sums[...] = jnp.zeros_like(sums)
    msg_b[...] = jnp.zeros_like(msg_b)

    def gather(base, buf):
        for e in range(EDGE_BLOCK):
            row = pl.multiple_of(src[base + e], 4)
            buf[4 * e : 4 * e + 4, :] = table[pl.ds(row, 4), :]

    def emit(base, half, buf):
        base = pl.multiple_of(base, EDGE_BLOCK)
        high, mid, low = split3(g8[:, pl.ds(base, EDGE_BLOCK)])
        g48 = jnp.concatenate([high, mid, low, high, mid, high], axis=0).astype(BF16)
        geo = dot_first(g48, w48[...])
        for j in range(4):
            lanes = slice(j * LANES, (j + 1) * LANES)
            v = buf[pl.ds(j, EDGE_BLOCK, stride=4), :] + geo[:, lanes]
            (msg_a, msg_b)[half][:, lanes] = silu(v).astype(BF16)

    def scatter(base, half):
        base = pl.multiple_of(jnp.maximum(base, 0), EDGE_BLOCK)
        select = one_hot(node[:, pl.ds(base, EDGE_BLOCK)], bands * rows)
        sums[...] += dot(select, (msg_a, msg_b)[half][...])

    blocks = edges // EDGE_BLOCK
    gather(0, buf_a)

    def step(t, carry):
        base = pl.multiple_of(t * (2 * EDGE_BLOCK), 2 * EDGE_BLOCK)
        gather(base + EDGE_BLOCK, buf_b)
        emit(base, 0, buf_a)
        scatter(base - EDGE_BLOCK, 1)
        gather(jnp.minimum(base + 2 * EDGE_BLOCK, (blocks - 1) * EDGE_BLOCK), buf_a)
        emit(base + EDGE_BLOCK, 1, buf_b)
        scatter(base, 0)
        return carry

    lax.fori_loop(0, blocks // 2, step, 0)
    scatter(edges - EDGE_BLOCK, 1)
    for which, out in enumerate((back2, back1, own, on1, on2)):
        out[...] = sums[which * rows : (which + 1) * rows, :].astype(out.dtype)


def band_sums(rows, *arrays):
    g2m_src, grid_in, w_in1 = arrays[:3]
    edges, nodes, width = g2m_src.shape[1], grid_in.shape[1], w_in1.shape[1]
    vmem = pl.BlockSpec(memory_space=pltpu.VMEM)
    hbm = pl.BlockSpec(memory_space=pltpu.HBM)
    return pl.pallas_call(
        message_kernel,
        out_shape=[jax.ShapeDtypeStruct((rows, width), dtype) for dtype in [BF16] * 5],
        in_specs=[hbm] * len(arrays),
        out_specs=[vmem] * 5,
        scratch_shapes=[pltpu.VMEM(a.shape, a.dtype) for a in arrays]
        + [
            pltpu.SMEM((edges,), jnp.int32),
            pltpu.VMEM((4 * nodes, LANES), F32),
            pltpu.VMEM((4 * EDGE_BLOCK, LANES), F32),
            pltpu.VMEM((4 * EDGE_BLOCK, LANES), F32),
            pltpu.VMEM((8, width), F32),
            pltpu.VMEM((8, edges), F32),
            pltpu.VMEM((48, width), BF16),
            pltpu.VMEM((width, width), BF16),
            pltpu.VMEM((EDGE_BLOCK, width), BF16),
            pltpu.VMEM((EDGE_BLOCK, width), BF16),
            pltpu.VMEM((5 * rows, width), F32),
            pltpu.SemaphoreType.DMA((len(arrays) + 4,)),
        ],
        compiler_params=pltpu.CompilerParams(vmem_limit_bytes=MESSAGE_VMEM),
        name="band_sums",
    )(*arrays)


def encoder_kernel(some, one, emb, w_enc1, b_enc, w_enc2, w_snd, lat, snd):
    total = some[...].astype(F32) + one[...].astype(F32)
    enc = silu(dot(total.astype(BF16), w_enc1[...]) + b_enc[...]).astype(BF16)
    mesh_lat = (emb[...].astype(F32) + dot(enc, w_enc2[...])).astype(BF16)
    lat[...] = mesh_lat
    snd[...] = dot(mesh_lat, w_snd[...]).astype(BF16)


def encoder(some, one, emb, w_enc1, b_enc, w_enc2, w_snd):
    vmem = pl.BlockSpec(memory_space=pltpu.VMEM)
    rows, width = emb.shape
    return pl.pallas_call(
        encoder_kernel,
        out_shape=[jax.ShapeDtypeStruct((rows, width), BF16)] * 2,
        in_specs=[vmem] * 7,
        out_specs=[vmem] * 2,
        compiler_params=pltpu.CompilerParams(vmem_limit_bytes=16 * 2**20),
        name="encoder",
    )(some, one, emb, w_enc1, b_enc.reshape(1, -1), w_enc2, w_snd)


def receiver_kernel(send, lat, w_rcv, w_edge, w_p1, w_p2, b_p, b_edge, w_p3, packed, packed32, offsets):
    offsets[...] = send[...] * 4
    rows, width = lat.shape
    packed[0:width, :] = dot(w_edge[...], w_p1[...]).astype(BF16)
    packed[width : 2 * width, :] = w_p3[...]
    packed[2 * width : 2 * width + rows, :] = lat[...]
    packed32[0:rows, :] = dot(lat[...], w_p2[...]) + b_p[...]
    packed32[rows : rows + 8, :] = jnp.broadcast_to(b_edge[...], (8, width))
    packed[2 * width + rows :, :] = dot(lat[...], w_rcv[...]).astype(BF16)


def receiver_side(send, lat, w_rcv, w_edge, w_p1, w_p2, b_p, b_edge, w_p3):
    vmem = pl.BlockSpec(memory_space=pltpu.VMEM)
    rows, width = lat.shape
    edges = send.shape[0]
    return pl.pallas_call(
        receiver_kernel,
        out_shape=[
            jax.ShapeDtypeStruct((2 * width + 2 * rows, width), BF16),
            jax.ShapeDtypeStruct((rows + 8, width), F32),
            jax.ShapeDtypeStruct((1, edges), jnp.int32),
        ],
        in_specs=[vmem] * 9,
        out_specs=[vmem] * 3,
        compiler_params=pltpu.CompilerParams(vmem_limit_bytes=12 * 2**20),
        cost_estimate=pl.CostEstimate(flops=10**9, bytes_accessed=6 * 10**6, transcendentals=0),
        name="receiver_side",
    )(
        send.reshape(1, -1), lat, w_rcv, w_edge, w_p1, w_p2,
        b_p.reshape(1, -1), b_edge.reshape(1, -1), w_p3,
    )


def processor_kernel(place, send, recv, packed, packed32, *refs):
    count, near = 10, NEAR_SHARDS
    out, shard, table, buf_a, buf_b, hid_a, hid_b, agg, sems = refs[count:]
    rows, width = out.shape
    lat = packed.at[2 * width : 2 * width + rows]
    receivers = packed.at[2 * width + rows : 2 * width + 2 * rows]
    copies = []
    for k in range(near, count):
        copies.append(pltpu.make_async_copy(refs[k], shard.at[k - near], sems.at[k - near]))
        copies[-1].start()
    agg[...] = jnp.zeros_like(agg)
    hid_b[...] = jnp.zeros_like(hid_b)
    b_edge = packed32[rows : rows + 1, :]
    for k in range(near):
        put_rows(table, place[k], refs[k][...].astype(F32) + b_edge)
    for k in range(near, count):
        copies[k - near].wait()
        put_rows(table, place[k], shard[k - near].astype(F32) + b_edge)

    def gather(base, buf):
        for e in range(EDGE_BLOCK):
            row = pl.multiple_of(send[0, base + e], 4)
            buf[4 * e : 4 * e + 4, :] = table[pl.ds(row, 4), :]

    def select(base):
        base = pl.multiple_of(base, EDGE_BLOCK)
        return one_hot(recv[:, pl.ds(base, EDGE_BLOCK)], rows)

    def emit(base, buf, hid):
        received = dot_first(select(base), receivers[...])
        for j in range(4):
            lanes = slice(j * LANES, (j + 1) * LANES)
            v = buf[pl.ds(j, EDGE_BLOCK, stride=4), :] + received[:, lanes]
            hid[:, lanes] = silu(v).astype(BF16)

    def add_up(base, hid):
        agg[...] += dot(select(jnp.maximum(base, 0)), hid[...])

    blocks = send.shape[1] // EDGE_BLOCK
    gather(0, buf_a)

    def step(t, carry):
        base = t * (2 * EDGE_BLOCK)
        gather(base + EDGE_BLOCK, buf_b)
        emit(base, buf_a, hid_a)
        add_up(base - EDGE_BLOCK, hid_b)
        gather(jnp.minimum(base + 2 * EDGE_BLOCK, (blocks - 1) * EDGE_BLOCK), buf_a)
        emit(base + EDGE_BLOCK, buf_b, hid_b)
        add_up(base, hid_a)
        return carry

    lax.fori_loop(0, blocks // 2, step, 0)
    add_up((blocks - 1) * EDGE_BLOCK, hid_b)
    node = dot(agg[...].astype(BF16), packed[0:width, :]) + packed32[0:rows, :]
    change = dot(silu(node).astype(BF16), packed[width : 2 * width, :])
    out[...] = (lat[...].astype(F32) + change).astype(BF16)


def processor(place, send, recv, packed, packed32, shards):
    vmem = pl.BlockSpec(memory_space=pltpu.VMEM)
    smem = pl.BlockSpec(memory_space=pltpu.SMEM)
    hbm = pl.BlockSpec(memory_space=pltpu.HBM)
    rows, width = shards[0].shape
    return pl.pallas_call(
        processor_kernel,
        out_shape=jax.ShapeDtypeStruct((rows, width), BF16),
        in_specs=[smem, smem] + [vmem] * (3 + NEAR_SHARDS) + [hbm] * (len(shards) - NEAR_SHARDS),
        out_specs=vmem,
        scratch_shapes=[
            pltpu.VMEM((len(shards) - NEAR_SHARDS, rows, width), BF16),
            pltpu.VMEM((4 * len(shards) * rows, LANES), F32),
            pltpu.VMEM((4 * EDGE_BLOCK, LANES), F32),
            pltpu.VMEM((4 * EDGE_BLOCK, LANES), F32),
            pltpu.VMEM((EDGE_BLOCK, width), BF16),
            pltpu.VMEM((EDGE_BLOCK, width), BF16),
            pltpu.VMEM((rows, width), F32),
            pltpu.SemaphoreType.DMA((len(shards) - NEAR_SHARDS,)),
        ],
        compiler_params=pltpu.CompilerParams(vmem_limit_bytes=PROCESSOR_VMEM),
        name="processor",
    )(place, send, recv.reshape(1, -1), packed, packed32, *shards)


def on_device(
    grid_in,
    g2m_geom,
    g2m_src,
    g2m_dst,
    g2m_node,
    mesh_emb,
    mesh_send,
    mesh_recv,
    w_in1,
    b_in,
    w_in2,
    w_g2m,
    w_geo,
    b_g2m,
    w_enc1,
    b_enc,
    w_enc2,
    w_snd,
    w_rcv,
    b_edge,
    w_edge,
    w_p1,
    w_p2,
    b_p,
    w_p3,
):
    groups, places = lax.axis_size("grp"), lax.axis_size("inner")
    bands = groups * places
    nodes_here = mesh_emb.shape[0]
    place = lax.axis_index("inner")
    core = place % 2

    def by_parity(even, odd):
        pairs = [(b, b + (odd if b % 2 else even)) for b in range(bands)]
        pairs = [pair for pair in pairs if 0 <= pair[1] < bands]
        return lambda value: lax.ppermute(value, BOTH, pairs)

    def onward(value):
        pairs = [(i, (i + (-2 if i % 2 else 2)) % places) for i in range(places)]
        return lax.ppermute(value, "inner", pairs)

    def across(value):
        return lax.ppermute(value, "inner", [(i, (i + 4) % places) for i in range(places)])

    def along_groups(value, by):
        pairs = [(i, i + by) for i in range(groups) if 0 <= i + by < groups]
        return lax.ppermute(value, "grp", pairs)

    other_core = by_parity(1, -1)

    turn = 1 - 2 * core
    back2, back1, own, on1, on2 = band_sums(
        nodes_here,
        g2m_src.reshape(1, -1),
        grid_in.T,
        w_in1,
        b_in.reshape(1, -1),
        w_in2,
        w_g2m,
        g2m_geom,
        w_geo,
        b_g2m.reshape(1, -1),
        g2m_dst.reshape(1, -1),
        g2m_node.reshape(1, -1),
    )
    crossing = other_core(back1)
    two = by_parity(-2, 2)(back2)
    joint = (on2.astype(F32) + crossing.astype(F32)).astype(BF16)
    one = by_parity(2, -2)(joint)
    on1, _ = lax.optimization_barrier((on1, joint))
    near = other_core(on1)
    some = own.astype(F32) + near.astype(F32) + two.astype(F32)
    mesh_lat, senders = encoder(some.astype(BF16), one, mesh_emb, w_enc1, b_enc, w_enc2, w_snd)

    partner = other_core(senders)
    next_a = onward(senders)
    far = across(senders)
    next_b = onward(partner)
    low = along_groups(senders, 1)
    high = along_groups(senders, -1)
    packed, packed32, offsets = receiver_side(
        mesh_send, mesh_lat, w_rcv, w_edge, w_p1, w_p2, b_p, b_edge, w_p3
    )
    next_a, offsets = lax.optimization_barrier((next_a, offsets))
    shards = [senders, partner, next_a, next_b, far]
    shards = shards + [other_core(shard) for shard in shards[2:]] + [low, high]
    before, after, opposite = [(place + by) % places for by in (-2 * turn, 2 * turn, 4)]
    where = [place, place + turn, before, before + turn, opposite]
    where = where + [after + turn, after, opposite + turn, places, places + 1]
    starts = jnp.stack([jnp.asarray(p, jnp.int32) for p in where]) * nodes_here
    return processor(starts, offsets, mesh_recv, packed, packed32, shards)


def solution(mesh):
    split = P(BOTH)
    rows = P(BOTH, None)
    return jax.shard_map(
        on_device,
        mesh=mesh,
        in_specs=(rows, P(None, BOTH), split, rows, split, rows, split, split) + (P(),) * 17,
        out_specs=rows,
        check_vma=False,
    )
```
